256 devices in a mesh: row: 64 (over y, z, x_hi), col: 4 (over x_lo, core).
Axes of the slice: x: 4 (x_hi: 2, x_lo: 2; x = x_hi * 2 + x_lo), y: 4, z: 8, core: 2. Of those that a mesh axis runs over, the one named last changes fastest.
Arguments:
- table: float32 [128, 1048576], P('col', 'row'), may hold values from -6 to 6
- signs: int32 [1048576], P('row'), may hold values from -1 to 1, as said below
- samples: int32 [8192], replicated, may hold values from 0 to 1048575
Outputs:
- sketch: float32 [128, 8192], P('col', 'row')
- gram: float32 [128, 128], replicated
The draws below stay inside these ranges and needn't reach their ends.
Inputs may be any that keep to these rules, and one draw needn't show every extreme that they name: `signs`: each entry is 1 or -1.
All inputs are finite; a program needn't handle non-finite values.
Results may differ from the reference program's by a relative error of at most 0.00016.
Values sent between devices are 32-bit elements; how exact they have to be, the bound alone decides.
A program may use at most 64 MiB of HBM per device.

```python
import jax
import jax.numpy as jnp
from jax import lax

C = 128
SAMPLES = 8192
ROWS = 1048576


def draw_signs(key, part):
    key = jax.random.fold_in(key, 1)
    return (2 * jax.random.randint(key, (ROWS,), 0, 2) - 1).astype(jnp.int32)


def plant(drawn, stream_key, low, largest):
    extent = drawn.shape
    spot = [jax.random.randint(jax.random.fold_in(stream_key, axis), (), 0, extent[axis]) for axis in range(len(extent))]
    drawn = drawn.at[tuple(spot)].set(low)
    longest = extent.index(max(extent))
    spot[longest] = (spot[longest] + 1) % extent[longest]
    return drawn.at[tuple(spot)].set(largest)


def steps_of(own_key, extent, pieces, least, largest):
    def one(axis_at, shards_of):
        heights = jax.random.uniform(jax.random.fold_in(jax.random.fold_in(own_key, 6), axis_at), (shards_of,), jnp.float32, least / len(pieces), largest / len(pieces))
        return jnp.repeat(jnp.exp(heights), extent[axis_at] // shards_of).reshape((-1,) + (1,) * (len(extent) - axis_at - 1))

    gain = one(*pieces[0])
    for cut in pieces[1:]:
        gain = gain * one(*cut)
    return gain


def centred(own_key, dims, scale, bound, cuts=(), dtype=jnp.bfloat16):
    result = scale * jax.random.normal(own_key, dims, jnp.float32)
    if cuts:
        result = result * steps_of(own_key, dims, cuts, -0.22, 0.18)
    return jnp.clip(result, -bound, bound).astype(dtype)


def setup_inputs(seed: int = 0) -> dict:
    seeds = jax.random.split(jax.random.key(seed), 4)
    table = centred(seeds[0], (C, ROWS), 1.0, 6.0, ((0, 4), (1, 64)), jnp.float32)
    signs = draw_signs(jax.random.fold_in(seeds[3], 71), 0)
    samples = plant(jax.random.randint(seeds[2], (SAMPLES,), 0, ROWS), jax.random.fold_in(seeds[2], 1), 0, ROWS - 1).astype(jnp.int32)
    return {"table": table, "signs": signs, "samples": samples}


def reference(table, signs, samples):
    signed = table * signs.astype(jnp.float32)[None, :]
    width = signed.shape[0]
    total = signed.shape[1]
    factor = jnp.float32(0.7071067811865476)
    stride = 1
    mixed = signed
    while stride < total:
        shaped = mixed.reshape(width, total // (2 * stride), 2, stride)
        first = shaped[:, :, 0, :]
        second = shaped[:, :, 1, :]
        mixed = jnp.stack(((first + second) * factor, (first - second) * factor), axis=2).reshape(width, total)
        stride = stride * 2
    sketch = jnp.take(mixed, samples, axis=1)
    gram = jnp.dot(sketch, sketch.T, precision=lax.Precision.HIGHEST, preferred_element_type=jnp.float32) / jnp.float32(SAMPLES)
    return sketch, gram
```

```python
import jax
import jax.numpy as jnp
from jax import lax
from jax.experimental import pallas as pl
from jax.experimental.pallas import tpu as pltpu
from jax.sharding import PartitionSpec as P

F32 = jnp.float32
BF16 = jnp.bfloat16
MESH = pl.DeviceIdType.MESH
NT = (((1,), (1,)), ((), ()))


def butterflies(parts):
    parts = list(parts)
    step = 1
    while step < len(parts):
        for i in range(len(parts)):
            if not i & step:
                a, b = parts[i], parts[i | step]
                parts[i], parts[i | step] = a + b, a - b
        step *= 2
    return parts


def parity(v):
    for shift in (4, 2, 1):
        v = v ^ (v >> shift)
    return v & 1


def split(p):
    a = p.astype(BF16)
    return a, (p - a.astype(F32)).astype(BF16)


def local_kernel(table, signs, samples, out, xs, hi, lo, rows_of, index_v, index_s, sem):
    me = lax.axis_index("row")
    index_v[...] = samples[...] & 16383
    copy = pltpu.make_async_copy(index_v, index_s, sem)
    copy.start()
    for h in range(2):
        rows = slice(16 * h, 16 * h + 16)
        for t in range(2):
            for w in range(8):
                parts = []
                for u in range(8):
                    col = u * 16 + w * 2 + t
                    parts.append(table[rows, col * 128:(col + 1) * 128] * signs[col:col + 1, :].astype(F32))
                for u, p in enumerate(butterflies(parts)):
                    col = u * 16 + w * 2 + t
                    xs[rows, col * 128:(col + 1) * 128] = p
            for u in range(8):
                cols = [u * 16 + w * 2 + t for w in range(8)]
                parts = [xs[rows, col * 128:(col + 1) * 128] for col in cols]
                for w, p in enumerate(butterflies(parts)):
                    a, b = split(p)
                    at = slice(u * 32 + 16 * h, u * 32 + 16 * h + 16)
                    hi[w, at, t * 128:(t + 1) * 128] = a
                    lo[w, at, t * 128:(t + 1) * 128] = b
    i = lax.broadcasted_iota(jnp.int32, (256, 256), 0)
    j = lax.broadcasted_iota(jnp.int32, (256, 256), 1)
    walsh = ((1 - 2 * parity(i & j)).astype(F32) * F32(1 / 1024)).astype(BF16)
    lane = lax.broadcasted_iota(jnp.int32, (256, 128), 1)
    below = [lane < 32, lane < 64, lane < 96]
    for w in range(8):
        done = lax.dot_general(walsh, hi[w], NT, preferred_element_type=F32)
        done = done + lax.dot_general(walsh, lo[w], NT, preferred_element_type=F32)
        for half in range(2):
            tile = done[:, half * 128:half * 128 + 128]
            rolled = [tile] + [pltpu.roll(tile, 32 * k, 1) for k in (1, 2, 3)]
            for x in range(4):
                r = [rolled[(g - x) % 4] for g in range(4)]
                four = jnp.where(below[0], r[0], jnp.where(below[1], r[1], jnp.where(below[2], r[2], r[3])))
                u = half * 4 + x
                rows_of[u * 2048 + w * 256:u * 2048 + w * 256 + 256, :] = four
    copy.wait()
    lane1 = lax.broadcasted_iota(jnp.int32, (1, 128), 1)
    below1 = [lane1 < 32, lane1 < 64, lane1 < 96]

    def chunk(q, carry):
        r = (q // 16) * 16 + (q % 8) * 2 + (q // 8) % 2
        for p in range(32):
            v = [rows_of[pl.ds(index_s[r, g * 32 + p], 1), :] for g in range(4)]
            four = jnp.where(below1[0], v[0], jnp.where(below1[1], v[1], jnp.where(below1[2], v[2], v[3])))
            out[pl.ds(q * 32 + p, 1), :] = four
        return carry

    lax.fori_loop(0, 64, chunk, 0)
    sign = (1 - 2 * parity((samples[...] >> 14) & me)).astype(F32)
    ti = lax.broadcasted_iota(jnp.int32, (32, 128), 1)
    pi = lax.broadcasted_iota(jnp.int32, (32, 128), 0)
    own = (ti & 31) == pi
    bi = lax.broadcasted_iota(jnp.int32, (128, 128), 0)
    bj = lax.broadcasted_iota(jnp.int32, (128, 128), 1)
    spread = ((bi >> 5) == (bj >> 5)).astype(BF16)
    for e in range(8):
        rs = [(e // 2) * 16 + z * 2 + e % 2 for z in range(8)]
        picked = jnp.concatenate([jnp.where(own, sign[r:r + 1, :], F32(0)) for r in rs], axis=0).astype(BF16)
        factor = jnp.dot(picked, spread, preferred_element_type=F32)
        out[e * 256:e * 256 + 256, :] = out[e * 256:e * 256 + 256, :] * factor


def exchange_kernel(terms, sketch, gram, r1, total, r2, whole, r3, r4, blocks, send, recv):
    row = lax.axis_index("row")
    col = lax.axis_index("col")
    y, z, x = row // 16, (row // 2) % 8, row % 2
    e = y * 2 + x

    def plane(k):
        other = (e + k) % 8
        return other, {"row": (other // 2) * 16 + z * 2 + other % 2}

    def line(k):
        other = (z + k) % 8
        return other, {"row": y * 16 + other * 2 + x}

    def column(k):
        return {"col": (col + k) % 4}

    barrier = pltpu.get_barrier_semaphore()
    for k in range(1, 8):
        pl.semaphore_signal(barrier, inc=1, device_id=plane(k)[1], device_id_type=MESH)
        pl.semaphore_signal(barrier, inc=1, device_id=line(k)[1], device_id_type=MESH)
    for k in range(1, 4):
        pl.semaphore_signal(barrier, inc=1, device_id=column(k), device_id_type=MESH)
    pl.semaphore_wait(barrier, 17)

    def start(src, dst, place, device):
        copy = pltpu.make_async_remote_copy(
            src_ref=src, dst_ref=dst, send_sem=send.at[place], recv_sem=recv.at[place], device_id=device, device_id_type=MESH
        )
        copy.start()
        return copy

    started = []

    def landed(copies):
        for copy in copies:
            copy.wait_recv()
        started.extend(copies)

    copies = []
    for k in range(1, 8):
        other, device = plane(k)
        copies.append(start(terms.at[pl.ds(other * 256, 256)], r1.at[k - 1], k - 1, device))
    landed(copies)
    acc = terms[pl.ds(pl.multiple_of(e * 256, 256), 256), :]
    for k in range(7):
        acc = acc + r1[k]
    total[...] = acc
    copies = []
    for k in range(1, 8):
        other, device = line(k)
        copies.append(start(total.at[pl.ds(other * 32, 32)], r2.at[k - 1], 7 + k - 1, device))
    landed(copies)
    acc = total[pl.ds(pl.multiple_of(z * 32, 32), 32), :]
    for k in range(7):
        acc = acc + r2[k]
    mine = jnp.concatenate([acc[:, g * 32:g * 32 + 32].T for g in range(4)], axis=1)
    sketch[...] = mine
    whole[col] = mine
    landed([start(whole.at[col], whole.at[col], 14 + k - 1, column(k)) for k in range(1, 4)])
    every = whole[...].reshape(128, 128)
    part = lax.dot_general(mine, every, NT, precision=lax.Precision.HIGHEST, preferred_element_type=F32)
    r3[e] = part
    landed([start(r3.at[e], r3.at[e], 17 + k - 1, plane(k)[1]) for k in range(1, 8)])
    acc = r3[0]
    for k in range(1, 8):
        acc = acc + r3[k]
    r4[z] = acc
    landed([start(r4.at[z], r4.at[z], 24 + k - 1, line(k)[1]) for k in range(1, 8)])
    acc = r4[0]
    for k in range(1, 8):
        acc = acc + r4[k]
    blocks[col] = acc * F32(1 / 8192)
    landed([start(blocks.at[col], blocks.at[col], 31 + k - 1, column(k)) for k in range(1, 4)])
    gram[...] = blocks[...].reshape(128, 128)
    for copy in started:
        copy.wait_send()


def per_device(table, signs, samples):
    vmem = pl.BlockSpec(memory_space=pltpu.VMEM)
    terms = pl.pallas_call(
        local_kernel,
        out_shape=jax.ShapeDtypeStruct((2048, 128), F32),
        in_specs=[vmem] * 3,
        out_specs=vmem,
        scratch_shapes=[
            pltpu.VMEM((32, 16384), F32),
            pltpu.VMEM((8, 256, 256), BF16),
            pltpu.VMEM((8, 256, 256), BF16),
            pltpu.VMEM((16384, 128), F32),
            pltpu.VMEM((64, 128), jnp.int32),
            pltpu.SMEM((64, 128), jnp.int32),
            pltpu.SemaphoreType.DMA,
        ],
        compiler_params=pltpu.CompilerParams(vmem_limit_bytes=40 * 2**20),
    )(table, signs.reshape(128, 128), samples.reshape(64, 128))
    return pl.pallas_call(
        exchange_kernel,
        out_shape=(jax.ShapeDtypeStruct((32, 128), F32), jax.ShapeDtypeStruct((128, 128), F32)),
        in_specs=[vmem],
        out_specs=(vmem, vmem),
        scratch_shapes=[
            pltpu.VMEM((7, 256, 128), F32),
            pltpu.VMEM((256, 128), F32),
            pltpu.VMEM((7, 32, 128), F32),
            pltpu.VMEM((4, 32, 128), F32),
            pltpu.VMEM((8, 32, 128), F32),
            pltpu.VMEM((8, 32, 128), F32),
            pltpu.VMEM((4, 32, 128), F32),
            pltpu.SemaphoreType.DMA((34,)),
            pltpu.SemaphoreType.DMA((34,)),
        ],
        compiler_params=pltpu.CompilerParams(
            collective_id=0, has_side_effects=True, vmem_limit_bytes=24 * 2**20
        ),
    )(terms)


def solution(mesh):
    return jax.shard_map(
        per_device,
        mesh=mesh,
        in_specs=(P("col", "row"), P("row"), P()),
        out_specs=(P("col", "row"), P()),
        check_vma=False,
    )
```

```python
import jax
import jax.numpy as jnp
from jax import lax
from jax.experimental import pallas as pl
from jax.experimental.pallas import tpu as pltpu
from jax.sharding import PartitionSpec as P

F32 = jnp.float32
BF16 = jnp.bfloat16
MESH = pl.DeviceIdType.MESH
NT = (((1,), (1,)), ((), ()))


def butterflies(parts):
    parts = list(parts)
    step = 1
    while step < len(parts):
        for i in range(len(parts)):
            if not i & step:
                a, b = parts[i], parts[i | step]
                parts[i], parts[i | step] = a + b, a - b
        step *= 2
    return parts


def parity(v):
    for shift in (4, 2, 1):
        v = v ^ (v >> shift)
    return v & 1


def split(p):
    a = p.astype(BF16)
    return a, (p - a.astype(F32)).astype(BF16)


def kernel(
    table_hbm, signs_hbm, samples_hbm, sketch, gram,
    table, signs, samples, xs, hi, lo, rows_of, index_v, index_s, sign_of, terms, r1, total, r2, whole, r3, r4, blocks,
    load, send, recv,
):
    row = lax.axis_index("row")
    col = lax.axis_index("col")
    y, z, x = row // 16, (row // 2) % 8, row % 2
    line_place = x * 4 + col

    def plane(dy, dx):
        return (y + dy) % 4, (x + dx) % 2

    def at(y, z, x):
        return {"row": y * 16 + z * 2 + x}

    def x_line(k):
        other = (line_place + k) % 8
        return {"row": y * 16 + z * 2 + other // 4, "col": other % 4}

    partners = [(2, 1), (1, 1), (3, 1), (2, 0), (0, 1), (1, 0), (3, 0)]
    copies_in = [
        pltpu.make_async_copy(signs_hbm, signs, load.at[0]),
        pltpu.make_async_copy(table_hbm.at[pl.ds(0, 16)], table.at[pl.ds(0, 16)], load.at[1]),
        pltpu.make_async_copy(samples_hbm, samples, load.at[2]),
        pltpu.make_async_copy(table_hbm.at[pl.ds(16, 16)], table.at[pl.ds(16, 16)], load.at[3]),
    ]
    for copy in copies_in:
        copy.start()
    barrier = pltpu.get_barrier_semaphore()
    met = [at(*(lambda o: (o[0], z, o[1]))(plane(dy, dx))) for dy, dx in partners]
    met += [at(y, (z + k) % 8, x) for k in range(1, 8)]
    met += [{"row": y * 16 + z * 2 + (x + dx) % 2, "col": (col + dc) % 4} for dx in range(2) for dc in range(1, 4)]
    for device in met:
        pl.semaphore_signal(barrier, inc=1, device_id=device, device_id_type=MESH)

    i = lax.broadcasted_iota(jnp.int32, (256, 256), 0)
    j = lax.broadcasted_iota(jnp.int32, (256, 256), 1)
    walsh = ((1 - 2 * parity(i & j)).astype(F32) * F32(1 / 1024)).astype(BF16)
    copies_in[0].wait()
    for h in range(2):
        rows = slice(16 * h, 16 * h + 16)
        copies_in[1 + 2 * h].wait()
        for t in range(2):
            for w in range(8):
                parts = []
                for u in range(8):
                    c = u * 16 + w * 2 + t
                    parts.append(table[rows, c * 128:(c + 1) * 128] * signs[c:c + 1, :].astype(F32))
                for u, p in enumerate(butterflies(parts)):
                    c = u * 16 + w * 2 + t
                    xs[rows, c * 128:(c + 1) * 128] = p
            for u in range(8):
                cs = [u * 16 + w * 2 + t for w in range(8)]
                parts = [xs[rows, c * 128:(c + 1) * 128] for c in cs]
                for w, p in enumerate(butterflies(parts)):
                    a, b = split(p)
                    put = slice(u * 32 + 16 * h, u * 32 + 16 * h + 16)
                    hi[w, put, t * 128:(t + 1) * 128] = a
                    lo[w, put, t * 128:(t + 1) * 128] = b
        if h == 0:
            copies_in[2].wait()
            index_v[...] = samples[...] & 16383
            index_copy = pltpu.make_async_copy(index_v, index_s, load.at[4])
            index_copy.start()
            sign_of[...] = (1 - 2 * parity((samples[...] >> 14) & row)).astype(F32)
    lane = lax.broadcasted_iota(jnp.int32, (256, 128), 1)
    below = [lane < 32, lane < 64, lane < 96]
    for w in range(8):
        done = lax.dot_general(walsh, hi[w], NT, preferred_element_type=F32)
        done = done + lax.dot_general(walsh, lo[w], NT, preferred_element_type=F32)
        for half in range(2):
            tile = done[:, half * 128:half * 128 + 128]
            rolled = [tile] + [pltpu.roll(tile, 32 * k, 1) for k in (1, 2, 3)]
            for v in range(4):
                r = [rolled[(g - v) % 4] for g in range(4)]
                four = jnp.where(below[0], r[0], jnp.where(below[1], r[1], jnp.where(below[2], r[2], r[3])))
                u = half * 4 + v
                rows_of[u * 2048 + w * 256:u * 2048 + w * 256 + 256, :] = four
    index_copy.wait()
    pl.semaphore_wait(barrier, len(met))

    lane1 = lax.broadcasted_iota(jnp.int32, (1, 128), 1)
    below1 = [lane1 < 32, lane1 < 64, lane1 < 96]
    own = (lax.broadcasted_iota(jnp.int32, (32, 128), 1) & 31) == lax.broadcasted_iota(jnp.int32, (32, 128), 0)
    spread = (
        (lax.broadcasted_iota(jnp.int32, (128, 128), 0) >> 5) == (lax.broadcasted_iota(jnp.int32, (128, 128), 1) >> 5)
    ).astype(BF16)

    def gather(slot, y_of, x_of):
        def chunk(q, carry):
            r = y_of * 16 + q * 2 + x_of
            base = slot * 256 + q * 32
            picked = jnp.where(own, sign_of[pl.ds(r, 1), :], F32(0)).astype(BF16)
            factor = jnp.dot(picked, spread, preferred_element_type=F32)
            for p in range(32):
                v = [rows_of[pl.ds(index_s[r, g * 32 + p], 1), :] for g in range(4)]
                four = jnp.where(below1[0], v[0], jnp.where(below1[1], v[1], jnp.where(below1[2], v[2], v[3])))
                terms[pl.ds(base + p, 1), :] = four
            here = pl.ds(pl.multiple_of(base, 32), 32)
            terms[here, :] = terms[here, :] * factor
            return carry

        lax.fori_loop(0, 8, chunk, 0)

    def start(src, dst, place, device):
        copy = pltpu.make_async_remote_copy(
            src_ref=src, dst_ref=dst, send_sem=send.at[place], recv_sem=recv.at[place], device_id=device, device_id_type=MESH
        )
        copy.start()
        return copy

    started = []

    def landed(copies):
        for copy in copies:
            copy.wait_recv()
        started.extend(copies)

    copies = []
    for k, (dy, dx) in enumerate(partners):
        y_of, x_of = plane(dy, dx)
        gather(k, y_of, x_of)
        copies.append(start(terms.at[pl.ds(k * 256, 256)], r1.at[k], k, at(y_of, z, x_of)))
    gather(7, y, x)
    landed(copies)
    acc = terms[7 * 256:8 * 256, :]
    for k in range(7):
        acc = acc + r1[k]
    total[...] = acc
    copies = []
    for k in (4, 3, 5, 2, 6, 1, 7):
        other = (z + k) % 8
        copies.append(start(total.at[pl.ds(other * 32, 32)], r2.at[k - 1], 7 + k - 1, at(y, other, x)))
    landed(copies)
    acc = total[pl.ds(pl.multiple_of(z * 32, 32), 32), :]
    for k in range(7):
        acc = acc + r2[k]
    mine = jnp.concatenate([acc[:, g * 32:g * 32 + 32].T for g in range(4)], axis=1)
    sketch[...] = mine
    whole[line_place] = mine
    landed([start(whole.at[line_place], whole.at[line_place], 14 + k - 1, x_line(k)) for k in range(1, 8)])
    part = jnp.zeros((16, 128), F32)
    for half in range(2):
        every = jnp.concatenate([whole[half * 4 + c] for c in range(4)], axis=0)
        left = whole[half * 4 + line_place // 2, pl.ds(pl.multiple_of((line_place % 2) * 16, 16), 16), :]
        part = part + lax.dot_general(left, every, NT, precision=lax.Precision.HIGHEST, preferred_element_type=F32)
    r3[y] = part
    landed([start(r3.at[y], r3.at[y], 21 + k - 1, at((y + k) % 4, z, x)) for k in (2, 1, 3)])
    acc = (r3[0] + r3[1]) + (r3[2] + r3[3])
    r4[z] = acc
    landed([start(r4.at[z], r4.at[z], 24 + k - 1, at(y, (z + k) % 8, x)) for k in (4, 3, 5, 2, 6, 1, 7)])
    acc = ((r4[0] + r4[1]) + (r4[2] + r4[3])) + ((r4[4] + r4[5]) + (r4[6] + r4[7]))
    blocks[line_place] = acc * F32(1 / 8192)
    landed([start(blocks.at[line_place], blocks.at[line_place], 31 + k - 1, x_line(k)) for k in range(1, 8)])
    gram[...] = blocks[...].reshape(128, 128)
    for copy in started:
        copy.wait_send()


def per_device(table, signs, samples):
    hbm = pl.BlockSpec(memory_space=pltpu.HBM)
    vmem = pl.BlockSpec(memory_space=pltpu.VMEM)
    return pl.pallas_call(
        kernel,
        out_shape=(jax.ShapeDtypeStruct((32, 128), F32), jax.ShapeDtypeStruct((128, 128), F32)),
        in_specs=[hbm] * 3,
        out_specs=(vmem, vmem),
        scratch_shapes=[
            pltpu.VMEM((32, 16384), F32),
            pltpu.VMEM((128, 128), jnp.int32),
            pltpu.VMEM((64, 128), jnp.int32),
            pltpu.VMEM((32, 16384), F32),
            pltpu.VMEM((8, 256, 256), BF16),
            pltpu.VMEM((8, 256, 256), BF16),
            pltpu.VMEM((16384, 128), F32),
            pltpu.VMEM((64, 128), jnp.int32),
            pltpu.SMEM((64, 128), jnp.int32),
            pltpu.VMEM((64, 128), F32),
            pltpu.VMEM((2048, 128), F32),
            pltpu.VMEM((7, 256, 128), F32),
            pltpu.VMEM((256, 128), F32),
            pltpu.VMEM((7, 32, 128), F32),
            pltpu.VMEM((8, 32, 128), F32),
            pltpu.VMEM((4, 16, 128), F32),
            pltpu.VMEM((8, 16, 128), F32),
            pltpu.VMEM((8, 16, 128), F32),
            pltpu.SemaphoreType.DMA((5,)),
            pltpu.SemaphoreType.DMA((38,)),
            pltpu.SemaphoreType.DMA((38,)),
        ],
        compiler_params=pltpu.CompilerParams(collective_id=0, has_side_effects=True, vmem_limit_bytes=40 * 2**20),
    )(table, signs.reshape(128, 128), samples.reshape(64, 128))


def solution(mesh):
    return jax.shard_map(
        per_device,
        mesh=mesh,
        in_specs=(P("col", "row"), P("row"), P()),
        out_specs=(P("col", "row"), P()),
        check_vma=False,
    )
```

```python
import jax
import jax.numpy as jnp
from jax import lax
from jax.experimental import pallas as pl
from jax.experimental.pallas import tpu as pltpu
from jax.sharding import PartitionSpec as P

F32 = jnp.float32
BF16 = jnp.bfloat16
MESH = pl.DeviceIdType.MESH
NT = (((1,), (1,)), ((), ()))


def butterflies(parts):
    parts = list(parts)
    step = 1
    while step < len(parts):
        for i in range(len(parts)):
            if not i & step:
                a, b = parts[i], parts[i | step]
                parts[i], parts[i | step] = a + b, a - b
        step *= 2
    return parts


def parity(v):
    for shift in (4, 2, 1):
        v = v ^ (v >> shift)
    return v & 1


def split(p):
    a = p.astype(BF16)
    return a, (p - a.astype(F32)).astype(BF16)


def kernel(
    table_hbm, signs_hbm, samples_hbm, sketch, gram,
    table, signs, samples, xs, hi, lo, rows_of, index_v, index_s, sign_of, terms_z, z1, total_z, z2, terms, r1, total, r2,
    whole, r3, r4, blocks,
    load, send, recv,
):
    row = lax.axis_index("row")
    col = lax.axis_index("col")
    y, z, x = row // 16, (row // 2) % 8, row % 2
    line_place = x * 4 + col

    def plane(dy, dx):
        return (y + dy) % 4, (x + dx) % 2

    def at(y, z, x):
        return {"row": y * 16 + z * 2 + x}

    def x_line(k):
        other = (line_place + k) % 8
        return {"row": y * 16 + z * 2 + other // 4, "col": other % 4}

    partners = [(2, 1), (1, 1), (3, 1), (2, 0), (0, 1), (1, 0), (3, 0)]
    copies_in = [
        pltpu.make_async_copy(signs_hbm, signs, load.at[0]),
        pltpu.make_async_copy(table_hbm.at[pl.ds(0, 16)], table.at[pl.ds(0, 16)], load.at[1]),
        pltpu.make_async_copy(samples_hbm, samples, load.at[2]),
        pltpu.make_async_copy(table_hbm.at[pl.ds(16, 16)], table.at[pl.ds(16, 16)], load.at[3]),
    ]
    for copy in copies_in:
        copy.start()
    barrier = pltpu.get_barrier_semaphore()
    met = [at(*(lambda o: (o[0], z, o[1]))(plane(dy, dx))) for dy, dx in partners]
    met += [at(y, (z + k) % 8, x) for k in range(1, 8)]
    met += [{"row": y * 16 + z * 2 + (x + dx) % 2, "col": (col + dc) % 4} for dx in range(2) for dc in range(1, 4)]
    for device in met:
        pl.semaphore_signal(barrier, inc=1, device_id=device, device_id_type=MESH)

    i = lax.broadcasted_iota(jnp.int32, (256, 256), 0)
    j = lax.broadcasted_iota(jnp.int32, (256, 256), 1)
    walsh = ((1 - 2 * parity(i & j)).astype(F32) * F32(1 / 1024)).astype(BF16)
    copies_in[0].wait()
    for h in range(2):
        rows = slice(16 * h, 16 * h + 16)
        copies_in[1 + 2 * h].wait()
        for t in range(2):
            for w in range(8):
                parts = []
                for u in range(8):
                    c = u * 16 + w * 2 + t
                    parts.append(table[rows, c * 128:(c + 1) * 128] * signs[c:c + 1, :].astype(F32))
                for u, p in enumerate(butterflies(parts)):
                    c = u * 16 + w * 2 + t
                    xs[rows, c * 128:(c + 1) * 128] = p
            for u in range(8):
                cs = [u * 16 + w * 2 + t for w in range(8)]
                parts = [xs[rows, c * 128:(c + 1) * 128] for c in cs]
                for w, p in enumerate(butterflies(parts)):
                    a, b = split(p)
                    put = slice(u * 32 + 16 * h, u * 32 + 16 * h + 16)
                    hi[w, put, t * 128:(t + 1) * 128] = a
                    lo[w, put, t * 128:(t + 1) * 128] = b
        if h == 0:
            copies_in[2].wait()
            index_v[...] = samples[...] & 16383
            index_copy = pltpu.make_async_copy(index_v, index_s, load.at[4])
            index_copy.start()
            sign_of[...] = (1 - 2 * parity((samples[...] >> 14) & row)).astype(F32)
    lane = lax.broadcasted_iota(jnp.int32, (256, 128), 1)
    below = [lane < 32, lane < 64, lane < 96]
    for w in range(8):
        done = lax.dot_general(walsh, hi[w], NT, preferred_element_type=F32)
        done = done + lax.dot_general(walsh, lo[w], NT, preferred_element_type=F32)
        for half in range(2):
            tile = done[:, half * 128:half * 128 + 128]
            rolled = [tile] + [pltpu.roll(tile, 32 * k, 1) for k in (1, 2, 3)]
            for v in range(4):
                r = [rolled[(g - v) % 4] for g in range(4)]
                four = jnp.where(below[0], r[0], jnp.where(below[1], r[1], jnp.where(below[2], r[2], r[3])))
                u = half * 4 + v
                rows_of[u * 2048 + w * 256:u * 2048 + w * 256 + 256, :] = four
    index_copy.wait()
    pl.semaphore_wait(barrier, len(met))

    lane1 = lax.broadcasted_iota(jnp.int32, (1, 128), 1)
    below1 = [lane1 < 32, lane1 < 64, lane1 < 96]
    spread = (
        (lax.broadcasted_iota(jnp.int32, (128, 128), 0) >> 5) == (lax.broadcasted_iota(jnp.int32, (128, 128), 1) >> 5)
    ).astype(BF16)

    def own(first, count):
        shape = (count, 128)
        return (lax.broadcasted_iota(jnp.int32, shape, 1) & 31) == lax.broadcasted_iota(jnp.int32, shape, 0) + first

    def gather(into, to, first, count, rs):
        mask = own(first, count)
        picked = [jnp.where(mask, sign_of[pl.ds(r, 1), :], F32(0)) for r in rs]
        factor = jnp.dot(jnp.concatenate(picked, axis=0).astype(BF16), spread, preferred_element_type=F32)
        for n, r in enumerate(rs):
            for p in range(count):
                v = [rows_of[pl.ds(index_s[r, g * 32 + first + p], 1), :] for g in range(4)]
                four = jnp.where(below1[0], v[0], jnp.where(below1[1], v[1], jnp.where(below1[2], v[2], v[3])))
                into[pl.ds(to + n * count + p, 1), :] = four
        here = pl.ds(pl.multiple_of(to, 8), len(rs) * count)
        into[here, :] = into[here, :] * factor

    def gather_z(n):
        _, other = line(n)

        def four(q, carry):
            gather(terms_z, n * 64 + q * 32, 0, 8, [(2 * q + e // 2) * 16 + other * 2 + e % 2 for e in range(4)])
            return carry

        lax.fori_loop(0, 2, four, 0)

    def gather_yx(n, s):
        y_of, x_of = turned(n)
        gather(terms, n * 192 + s * 48, 8, 24, [y_of * 16 + (2 * s + j) * 2 + x_of for j in range(2)])

    def line(n):
        k = jnp.where(n == 7, 0, (n + 4) % 8 + n // 4)
        return k, (z + k) % 8

    def turned(n):
        return (y + (7 - n) // 2) % 4, (x + (7 - n) % 2) % 2

    def remote(src, dst, place, device):
        return pltpu.make_async_remote_copy(
            src_ref=src, dst_ref=dst, send_sem=send.at[place], recv_sem=recv.at[place], device_id=device, device_id_type=MESH
        )

    def start(src, dst, place, device):
        copy = remote(src, dst, place, device)
        copy.start()
        return copy

    def sent_z(n):
        return remote(terms_z.at[pl.ds(n * 64, 64)], z1.at[n], n, at(y, line(n)[1], x))

    def sent_yx(n, s):
        y_of, x_of = turned(n)
        return remote(terms.at[pl.ds(n * 192 + s * 48, 48)], r1.at[n, pl.ds(s * 48, 48)], 7 + n * 4 + s, at(y_of, z, x_of))

    started = []

    def landed(copies):
        for copy in copies:
            copy.wait_recv()
        started.extend(copies)

    def added(own_part, slots):
        acc = own_part
        for k in range(7):
            acc = acc + slots[k]
        return acc

    def step(s, carry):
        def of_z(n, carry):
            gather_z(n)
            sent_z(n).start()
            return carry

        def of_yx(n, carry):
            gather_yx(n, s)
            sent_yx(n, s).start()
            return carry

        lax.fori_loop(2 * s, jnp.minimum(2 * s + 2, 7), of_z, 0)
        lax.fori_loop(0, 7, of_yx, 0)
        return carry

    lax.fori_loop(0, 4, step, 0)
    gather_z(7)

    def of_own(s, carry):
        gather_yx(7, s)
        return carry

    lax.fori_loop(0, 4, of_own, 0)
    landed([sent_z(n) for n in range(7)])
    total_z[...] = added(terms_z[7 * 64:8 * 64, :], z1)
    copies_z = []
    for n in range(7):
        y_of, x_of = turned(n)
        copies_z.append(start(total_z.at[pl.ds((y_of * 2 + x_of) * 8, 8)], z2.at[n], 35 + n, at(y_of, z, x_of)))
    landed([sent_yx(n, s) for s in range(4) for n in range(7)])
    total[...] = added(terms[7 * 192:8 * 192, :], r1)
    copies = []
    for n in range(7):
        other = line(n)[1]
        copies.append(start(total.at[pl.ds(other * 24, 24)], r2.at[n], 42 + n, at(y, other, x)))
    landed(copies_z)
    acc_z = added(total_z[pl.ds(pl.multiple_of((y * 2 + x) * 8, 8), 8), :], z2)
    landed(copies)
    acc = jnp.concatenate([acc_z, added(total[pl.ds(pl.multiple_of(z * 24, 8), 24), :], r2)], axis=0)
    mine = jnp.concatenate([acc[:, g * 32:g * 32 + 32].T for g in range(4)], axis=1)
    sketch[...] = mine
    whole[line_place] = mine
    landed([start(whole.at[line_place], whole.at[line_place], 49 + k - 1, x_line(k)) for k in range(1, 8)])
    part = jnp.zeros((16, 128), F32)
    for half in range(2):
        every = jnp.concatenate([whole[half * 4 + c] for c in range(4)], axis=0)
        left = whole[half * 4 + line_place // 2, pl.ds(pl.multiple_of((line_place % 2) * 16, 16), 16), :]
        part = part + lax.dot_general(left, every, NT, precision=lax.Precision.HIGHEST, preferred_element_type=F32)
    r3[y] = part
    landed([start(r3.at[y], r3.at[y], 56 + k - 1, at((y + k) % 4, z, x)) for k in (2, 1, 3)])
    acc = (r3[0] + r3[1]) + (r3[2] + r3[3])
    r4[z] = acc
    landed([start(r4.at[z], r4.at[z], 59 + k - 1, at(y, (z + k) % 8, x)) for k in (4, 3, 5, 2, 6, 1, 7)])
    acc = ((r4[0] + r4[1]) + (r4[2] + r4[3])) + ((r4[4] + r4[5]) + (r4[6] + r4[7]))
    blocks[line_place] = acc * F32(1 / 8192)
    landed([start(blocks.at[line_place], blocks.at[line_place], 66 + k - 1, x_line(k)) for k in range(1, 8)])
    gram[...] = blocks[...].reshape(128, 128)
    for copy in started:
        copy.wait_send()


def per_device(table, signs, samples):
    hbm = pl.BlockSpec(memory_space=pltpu.HBM)
    vmem = pl.BlockSpec(memory_space=pltpu.VMEM)
    return pl.pallas_call(
        kernel,
        out_shape=(jax.ShapeDtypeStruct((32, 128), F32), jax.ShapeDtypeStruct((128, 128), F32)),
        in_specs=[hbm] * 3,
        out_specs=(vmem, vmem),
        scratch_shapes=[
            pltpu.VMEM((32, 16384), F32),
            pltpu.VMEM((128, 128), jnp.int32),
            pltpu.VMEM((64, 128), jnp.int32),
            pltpu.VMEM((32, 16384), F32),
            pltpu.VMEM((8, 256, 256), BF16),
            pltpu.VMEM((8, 256, 256), BF16),
            pltpu.VMEM((16384, 128), F32),
            pltpu.VMEM((64, 128), jnp.int32),
            pltpu.SMEM((64, 128), jnp.int32),
            pltpu.VMEM((64, 128), F32),
            pltpu.VMEM((512, 128), F32),
            pltpu.VMEM((7, 64, 128), F32),
            pltpu.VMEM((64, 128), F32),
            pltpu.VMEM((7, 8, 128), F32),
            pltpu.VMEM((1536, 128), F32),
            pltpu.VMEM((7, 192, 128), F32),
            pltpu.VMEM((192, 128), F32),
            pltpu.VMEM((7, 24, 128), F32),
            pltpu.VMEM((8, 32, 128), F32),
            pltpu.VMEM((4, 16, 128), F32),
            pltpu.VMEM((8, 16, 128), F32),
            pltpu.VMEM((8, 16, 128), F32),
            pltpu.SemaphoreType.DMA((5,)),
            pltpu.SemaphoreType.DMA((73,)),
            pltpu.SemaphoreType.DMA((73,)),
        ],
        compiler_params=pltpu.CompilerParams(collective_id=0, has_side_effects=True, vmem_limit_bytes=62 * 2**20),
    )(table, signs.reshape(128, 128), samples.reshape(64, 128))


def solution(mesh):
    return jax.shard_map(
        per_device,
        mesh=mesh,
        in_specs=(P("col", "row"), P("row"), P()),
        out_specs=(P("col", "row"), P()),
        check_vma=False,
    )
```

```python
import jax
import jax.numpy as jnp
from jax import lax
from jax.experimental import pallas as pl
from jax.experimental.pallas import tpu as pltpu
from jax.sharding import PartitionSpec as P

F32 = jnp.float32
BF16 = jnp.bfloat16
MESH = pl.DeviceIdType.MESH
NT = (((1,), (1,)), ((), ()))
FIRST = 8


def butterflies(parts):
    parts = list(parts)
    step = 1
    while step < len(parts):
        for i in range(len(parts)):
            if not i & step:
                a, b = parts[i], parts[i | step]
                parts[i], parts[i | step] = a + b, a - b
        step *= 2
    return parts


def parity(v):
    for shift in (4, 2, 1):
        v = v ^ (v >> shift)
    return v & 1


def split(p):
    a = p.astype(BF16)
    return a, (p - a.astype(F32)).astype(BF16)


def kernel(
    table_hbm, signs_hbm, samples_hbm, sketch, gram,
    table, signs, flips, samples, xs, hi, lo, rows_of, index_v, index_s, sign_of, terms_z, z1, total_z, z2, terms, r1, total, r2,
    whole, r3, r4, blocks,
    load, send, recv,
):
    row = lax.axis_index("row")
    col = lax.axis_index("col")
    y, z, x = row // 16, (row // 2) % 8, row % 2
    line_place = x * 4 + col

    def at(y, z, x):
        return {"row": y * 16 + z * 2 + x}

    def x_line(k):
        other = (line_place + k) % 8
        return {"row": y * 16 + z * 2 + other // 4, "col": other % 4}

    partners = [(2, 1), (1, 1), (3, 1), (2, 0), (0, 1), (1, 0), (3, 0)]
    copies_in = [
        pltpu.make_async_copy(signs_hbm, signs, load.at[0]),
        pltpu.make_async_copy(table_hbm.at[pl.ds(0, 16)], table.at[pl.ds(0, 16)], load.at[1]),
        pltpu.make_async_copy(samples_hbm, samples, load.at[2]),
        pltpu.make_async_copy(table_hbm.at[pl.ds(16, 16)], table.at[pl.ds(16, 16)], load.at[3]),
    ]
    for copy in copies_in:
        copy.start()
    barrier = pltpu.get_barrier_semaphore()
    met = [at(y, (z + k) % 8, x) for k in (4, 3, 5, 2, 6, 1, 7)]
    met += [at((y + dy) % 4, z, (x + dx) % 2) for dy, dx in partners]
    met += [{"row": y * 16 + z * 2 + (x + dx) % 2, "col": (col + dc) % 4} for dx in range(2) for dc in range(1, 4)]
    for device in met:
        pl.semaphore_signal(barrier, inc=1, device_id=device, device_id_type=MESH)

    i = lax.broadcasted_iota(jnp.int32, (256, 256), 0)
    j = lax.broadcasted_iota(jnp.int32, (256, 256), 1)
    walsh = ((1 - 2 * parity(i & j)).astype(F32) * F32(1 / 1024)).astype(BF16)
    copies_in[0].wait()
    flips[...] = signs[...].astype(F32)
    for h in range(2):
        rows = slice(16 * h, 16 * h + 16)
        copies_in[1 + 2 * h].wait()
        for t in range(2):
            for w in range(8):
                parts = []
                for u in range(8):
                    c = u * 16 + w * 2 + t
                    parts.append(table[rows, c * 128:(c + 1) * 128] * flips[c:c + 1, :])
                for u, p in enumerate(butterflies(parts)):
                    c = u * 16 + w * 2 + t
                    xs[rows, c * 128:(c + 1) * 128] = p
            for u in range(8):
                cs = [u * 16 + w * 2 + t for w in range(8)]
                parts = [xs[rows, c * 128:(c + 1) * 128] for c in cs]
                for w, p in enumerate(butterflies(parts)):
                    a, b = split(p)
                    put = slice(u * 32 + 16 * h, u * 32 + 16 * h + 16)
                    hi[w, put, t * 128:(t + 1) * 128] = a
                    lo[w, put, t * 128:(t + 1) * 128] = b
        if h == 0:
            copies_in[2].wait()
            local = samples[...] & 16383
            group = lax.broadcasted_iota(jnp.int32, (64, 128), 1) >> 5
            turn = (group - (local >> 11)) & 3
            index_v[...] = turn * 4096 + (local >> 13) * 2048 + (local & 2047)
            index_copy = pltpu.make_async_copy(index_v, index_s, load.at[4])
            index_copy.start()
            sign_of[...] = (1 - 2 * parity((samples[...] >> 14) & row)).astype(F32)
    for w in range(8):
        done = lax.dot_general(walsh, hi[w], NT, preferred_element_type=F32)
        done = done + lax.dot_general(walsh, lo[w], NT, preferred_element_type=F32)
        for half in range(2):
            tile = done[:, half * 128:half * 128 + 128]
            for k in range(4):
                put = k * 4096 + half * 2048 + w * 256
                rows_of[put:put + 256, :] = pltpu.roll(tile, 32 * k, 1) if k else tile
    index_copy.wait()
    pl.semaphore_wait(barrier, len(met))

    lane1 = lax.broadcasted_iota(jnp.int32, (1, 128), 1)
    below1 = [lane1 < 32, lane1 < 64, lane1 < 96]
    spread = (
        (lax.broadcasted_iota(jnp.int32, (128, 128), 0) >> 5) == (lax.broadcasted_iota(jnp.int32, (128, 128), 1) >> 5)
    ).astype(BF16)

    def gather(into, places, first, count, rs):
        padded = -(-count // 8) * 8
        mask = (lax.broadcasted_iota(jnp.int32, (padded, 128), 1) & 31) == (
            lax.broadcasted_iota(jnp.int32, (padded, 128), 0) + first
        )
        picked = [jnp.where(mask, sign_of[pl.ds(r, 1), :], F32(0)) for r in rs]
        factor = jnp.dot(jnp.concatenate(picked, axis=0).astype(BF16), spread, preferred_element_type=F32)
        for place, r in zip(places, rs):
            for p in range(count):
                v = [rows_of[pl.ds(index_s[r, g * 32 + first + p], 1), :] for g in range(4)]
                four = jnp.where(below1[0], v[0], jnp.where(below1[1], v[1], jnp.where(below1[2], v[2], v[3])))
                into[place + (pl.ds(p, 1), slice(None))] = four
        for i, place in enumerate(places):
            into[place] = into[place] * factor[i * padded:i * padded + count]

    def gather_z(n):
        _, other = line(n)

        def four(q, carry):
            gather(terms_z, [(n, q * 4 + e) for e in range(4)], 0, FIRST, [(2 * q + e // 2) * 16 + other * 2 + e % 2 for e in range(4)])
            return carry

        lax.fori_loop(0, 2, four, 0)

    def gather_yx(n, s):
        y_of, x_of = turned(n)
        gather(terms, [(n, 2 * s + j) for j in range(2)], FIRST, 32 - FIRST, [y_of * 16 + (2 * s + j) * 2 + x_of for j in range(2)])

    def line(n):
        k = jnp.where(n == 7, 0, (n + 4) % 8 + n // 4)
        return k, (z + k) % 8

    def turned(n):
        return (y + (7 - n) // 2) % 4, (x + (7 - n) % 2) % 2

    def remote(src, dst, place, device):
        return pltpu.make_async_remote_copy(
            src_ref=src, dst_ref=dst, send_sem=send.at[place], recv_sem=recv.at[place], device_id=device, device_id_type=MESH
        )

    def start(src, dst, place, device):
        copy = remote(src, dst, place, device)
        copy.start()
        return copy

    def sent_z(n):
        return remote(terms_z.at[n], z1.at[n], n, at(y, line(n)[1], x))

    def sent_yx(n, s):
        y_of, x_of = turned(n)
        return remote(terms.at[n, pl.ds(2 * s, 2)], r1.at[n, pl.ds(2 * s, 2)], 7 + n * 4 + s, at(y_of, z, x_of))

    started = []

    def landed(copies):
        for copy in copies:
            copy.wait_recv()
        started.extend(copies)

    def added(own_part, slots):
        acc = own_part
        for k in range(7):
            acc = acc + slots[k]
        return acc

    def step(s, carry):
        def of_z(n, carry):
            gather_z(n)
            sent_z(n).start()
            return carry

        def of_yx(n, carry):
            gather_yx(n, s)
            sent_yx(n, s).start()
            return carry

        lax.fori_loop(jnp.where(s == 0, 0, jnp.minimum(2 * s + 1, 7)), jnp.minimum(2 * s + 3, 7), of_z, 0)
        lax.fori_loop(0, 7, of_yx, 0)
        return carry

    lax.fori_loop(0, 4, step, 0)
    gather_z(7)

    def of_own(s, carry):
        gather_yx(7, s)
        return carry

    lax.fori_loop(0, 4, of_own, 0)
    landed([sent_z(n) for n in range(7)])
    total_z[...] = added(terms_z[7], z1)
    copies_z = []
    for n in range(7):
        y_of, x_of = turned(n)
        copies_z.append(start(total_z.at[y_of * 2 + x_of], z2.at[n], 35 + n, at(y_of, z, x_of)))
    landed([sent_yx(n, s) for s in range(4) for n in range(7)])
    total[...] = added(terms[7], r1)
    copies = []
    for n in range(7):
        other = line(n)[1]
        copies.append(start(total.at[other], r2.at[n], 42 + n, at(y, other, x)))
    landed(copies_z)
    acc_z = added(total_z[y * 2 + x], z2)
    landed(copies)
    acc = jnp.concatenate([acc_z, added(total[z], r2)], axis=0)
    mine = jnp.concatenate([acc[:, g * 32:g * 32 + 32].T for g in range(4)], axis=1)
    sketch[...] = mine
    whole[line_place] = mine
    landed([start(whole.at[line_place], whole.at[line_place], 49 + k - 1, x_line(k)) for k in range(1, 8)])
    part = jnp.zeros((16, 128), F32)
    for half in range(2):
        every = jnp.concatenate([whole[half * 4 + c] for c in range(4)], axis=0)
        left = whole[half * 4 + line_place // 2, pl.ds(pl.multiple_of((line_place % 2) * 16, 16), 16), :]
        part = part + lax.dot_general(left, every, NT, precision=lax.Precision.HIGHEST, preferred_element_type=F32)
    r3[y] = part
    landed([start(r3.at[y], r3.at[y], 56 + k - 1, at((y + k) % 4, z, x)) for k in (2, 1, 3)])
    acc = (r3[0] + r3[1]) + (r3[2] + r3[3])
    r4[z] = acc
    landed([start(r4.at[z], r4.at[z], 59 + k - 1, at(y, (z + k) % 8, x)) for k in (4, 3, 5, 2, 6, 1, 7)])
    acc = ((r4[0] + r4[1]) + (r4[2] + r4[3])) + ((r4[4] + r4[5]) + (r4[6] + r4[7]))
    blocks[line_place] = acc * F32(1 / 8192)
    landed([start(blocks.at[line_place], blocks.at[line_place], 66 + k - 1, x_line(k)) for k in range(1, 8)])
    gram[...] = blocks[...].reshape(128, 128)
    for copy in started:
        copy.wait_send()


def per_device(table, signs, samples):
    hbm = pl.BlockSpec(memory_space=pltpu.HBM)
    vmem = pl.BlockSpec(memory_space=pltpu.VMEM)
    return pl.pallas_call(
        kernel,
        out_shape=(jax.ShapeDtypeStruct((32, 128), F32), jax.ShapeDtypeStruct((128, 128), F32)),
        in_specs=[hbm] * 3,
        out_specs=(vmem, vmem),
        scratch_shapes=[
            pltpu.VMEM((32, 16384), F32),
            pltpu.VMEM((128, 128), jnp.int32),
            pltpu.VMEM((128, 128), F32),
            pltpu.VMEM((64, 128), jnp.int32),
            pltpu.VMEM((32, 16384), F32),
            pltpu.VMEM((8, 256, 256), BF16),
            pltpu.VMEM((8, 256, 256), BF16),
            pltpu.VMEM((16384, 128), F32),
            pltpu.VMEM((64, 128), jnp.int32),
            pltpu.SMEM((64, 128), jnp.int32),
            pltpu.VMEM((64, 128), F32),
            pltpu.VMEM((8, 8, FIRST, 128), F32),
            pltpu.VMEM((7, 8, FIRST, 128), F32),
            pltpu.VMEM((8, FIRST, 128), F32),
            pltpu.VMEM((7, FIRST, 128), F32),
            pltpu.VMEM((8, 8, 32 - FIRST, 128), F32),
            pltpu.VMEM((7, 8, 32 - FIRST, 128), F32),
            pltpu.VMEM((8, 32 - FIRST, 128), F32),
            pltpu.VMEM((7, 32 - FIRST, 128), F32),
            pltpu.VMEM((8, 32, 128), F32),
            pltpu.VMEM((4, 16, 128), F32),
            pltpu.VMEM((8, 16, 128), F32),
            pltpu.VMEM((8, 16, 128), F32),
            pltpu.SemaphoreType.DMA((5,)),
            pltpu.SemaphoreType.DMA((73,)),
            pltpu.SemaphoreType.DMA((73,)),
        ],
        compiler_params=pltpu.CompilerParams(collective_id=0, has_side_effects=True, vmem_limit_bytes=55104 * 2**10),
    )(table, signs.reshape(128, 128), samples.reshape(64, 128))


def solution(mesh):
    return jax.shard_map(
        per_device,
        mesh=mesh,
        in_specs=(P("col", "row"), P("row"), P()),
        out_specs=(P("col", "row"), P()),
        check_vma=False,
    )
```

```python
import jax
import jax.numpy as jnp
from jax import lax
from jax.experimental import pallas as pl
from jax.experimental.pallas import tpu as pltpu
from jax.sharding import PartitionSpec as P

F32 = jnp.float32
BF16 = jnp.bfloat16
MESH = pl.DeviceIdType.MESH
NT = (((1,), (1,)), ((), ()))
FIRST = 8


def butterflies(parts):
    parts = list(parts)
    step = 1
    while step < len(parts):
        for i in range(len(parts)):
            if not i & step:
                a, b = parts[i], parts[i | step]
                parts[i], parts[i | step] = a + b, a - b
        step *= 2
    return parts


def parity(v):
    for shift in (4, 2, 1):
        v = v ^ (v >> shift)
    return v & 1


def split(p):
    a = p.astype(BF16)
    return a, (p - a.astype(F32)).astype(BF16)


def kernel(
    table_hbm, signs_hbm, samples_hbm, sketch, gram,
    table, signs, flips, samples, xs, hi, lo, rows_of, index_v, index_s, sign_of, terms_z, z1, total_z, z2, terms, r1, total, r2,
    whole, r3, r4, blocks,
    load, send, recv,
):
    row = lax.axis_index("row")
    col = lax.axis_index("col")
    y, z, x = row // 16, (row // 2) % 8, row % 2
    line_place = x * 4 + col

    def at(y, z, x):
        return {"row": y * 16 + z * 2 + x}

    def x_line(k):
        other = (line_place + k) % 8
        return {"row": y * 16 + z * 2 + other // 4, "col": other % 4}

    partners = [(2, 1), (1, 1), (3, 1), (2, 0), (0, 1), (1, 0), (3, 0)]
    copies_in = [
        pltpu.make_async_copy(signs_hbm, signs, load.at[0]),
        pltpu.make_async_copy(table_hbm.at[pl.ds(0, 8)], table.at[pl.ds(0, 8)], load.at[1]),
        pltpu.make_async_copy(table_hbm.at[pl.ds(8, 8)], table.at[pl.ds(8, 8)], load.at[2]),
        pltpu.make_async_copy(samples_hbm, samples, load.at[3]),
        pltpu.make_async_copy(table_hbm.at[pl.ds(16, 8)], table.at[pl.ds(16, 8)], load.at[4]),
        pltpu.make_async_copy(table_hbm.at[pl.ds(24, 8)], table.at[pl.ds(24, 8)], load.at[5]),
    ]
    for copy in copies_in:
        copy.start()
    barrier = pltpu.get_barrier_semaphore()
    met = [at(y, (z + k) % 8, x) for k in (4, 3, 5, 2, 6, 1, 7)]
    met += [at((y + dy) % 4, z, (x + dx) % 2) for dy, dx in partners]
    met += [{"row": y * 16 + z * 2 + (x + dx) % 2, "col": (col + dc) % 4} for dx in range(2) for dc in range(1, 4)]
    for device in met:
        pl.semaphore_signal(barrier, inc=1, device_id=device, device_id_type=MESH)

    i = lax.broadcasted_iota(jnp.int32, (256, 256), 0)
    j = lax.broadcasted_iota(jnp.int32, (256, 256), 1)
    walsh = ((1 - 2 * parity(i & j)).astype(F32) * F32(1 / 1024)).astype(BF16)
    copies_in[0].wait()
    flips[...] = signs[...].astype(F32)
    for h in range(2):
        rows = slice(16 * h, 16 * h + 16)
        copies_in[1 + 3 * h].wait()
        copies_in[2 + 3 * h].wait()
        for t in range(2):
            for w in range(8):
                parts = []
                for u in range(8):
                    c = u * 16 + w * 2 + t
                    parts.append(table[rows, c * 128:(c + 1) * 128] * flips[c:c + 1, :])
                for u, p in enumerate(butterflies(parts)):
                    c = u * 16 + w * 2 + t
                    xs[rows, c * 128:(c + 1) * 128] = p
            for u in range(8):
                cs = [u * 16 + w * 2 + t for w in range(8)]
                parts = [xs[rows, c * 128:(c + 1) * 128] for c in cs]
                for w, p in enumerate(butterflies(parts)):
                    a, b = split(p)
                    put = slice(u * 32 + 16 * h, u * 32 + 16 * h + 16)
                    hi[w, put, t * 128:(t + 1) * 128] = a
                    lo[w, put, t * 128:(t + 1) * 128] = b
        if h == 0:
            copies_in[3].wait()
            local = samples[...] & 16383
            group = lax.broadcasted_iota(jnp.int32, (64, 128), 1) >> 5
            turn = (group - (local >> 11)) & 3
            index_v[...] = turn * 4096 + (local >> 13) * 2048 + (local & 2047)
            index_copy = pltpu.make_async_copy(index_v, index_s, load.at[6])
            index_copy.start()
            sign_of[...] = (1 - 2 * parity((samples[...] >> 14) & row)).astype(F32)
    for w in range(8):
        done = lax.dot_general(walsh, hi[w], NT, preferred_element_type=F32)
        done = done + lax.dot_general(walsh, lo[w], NT, preferred_element_type=F32)
        for half in range(2):
            tile = done[:, half * 128:half * 128 + 128]
            for k in range(4):
                put = k * 4096 + half * 2048 + w * 256
                rows_of[put:put + 256, :] = pltpu.roll(tile, 32 * k, 1) if k else tile
    index_copy.wait()
    pl.semaphore_wait(barrier, len(met))

    lane1 = lax.broadcasted_iota(jnp.int32, (1, 128), 1)
    below1 = [lane1 < 32, lane1 < 64, lane1 < 96]
    spread = (
        (lax.broadcasted_iota(jnp.int32, (128, 128), 0) >> 5) == (lax.broadcasted_iota(jnp.int32, (128, 128), 1) >> 5)
    ).astype(BF16)

    def gather(into, places, first, count, rs):
        padded = -(-count // 8) * 8
        mask = (lax.broadcasted_iota(jnp.int32, (padded, 128), 1) & 31) == (
            lax.broadcasted_iota(jnp.int32, (padded, 128), 0) + first
        )
        picked = [jnp.where(mask, sign_of[pl.ds(r, 1), :], F32(0)) for r in rs]
        factor = jnp.dot(jnp.concatenate(picked, axis=0).astype(BF16), spread, preferred_element_type=F32)
        for place, r in zip(places, rs):
            for p in range(count):
                v = [rows_of[pl.ds(index_s[r, g * 32 + first + p], 1), :] for g in range(4)]
                four = jnp.where(below1[0], v[0], jnp.where(below1[1], v[1], jnp.where(below1[2], v[2], v[3])))
                into[place + (pl.ds(p, 1), slice(None))] = four
        for i, place in enumerate(places):
            into[place] = into[place] * factor[i * padded:i * padded + count]

    def gather_z(n):
        _, other = line(n)

        def four(q, carry):
            gather(terms_z, [(n, q * 4 + e) for e in range(4)], 0, FIRST, [(2 * q + e // 2) * 16 + other * 2 + e % 2 for e in range(4)])
            return carry

        lax.fori_loop(0, 2, four, 0)

    def gather_yx(n, s):
        y_of, x_of = turned(n)
        gather(terms, [(n, 2 * s + j) for j in range(2)], FIRST, 32 - FIRST, [y_of * 16 + (2 * s + j) * 2 + x_of for j in range(2)])

    def line(n):
        k = jnp.where(n == 7, 0, (n + 4) % 8 + n // 4)
        return k, (z + k) % 8

    def turned(n):
        return (y + (7 - n) // 2) % 4, (x + (7 - n) % 2) % 2

    def remote(src, dst, place, device):
        return pltpu.make_async_remote_copy(
            src_ref=src, dst_ref=dst, send_sem=send.at[place], recv_sem=recv.at[place], device_id=device, device_id_type=MESH
        )

    def start(src, dst, place, device):
        copy = remote(src, dst, place, device)
        copy.start()
        return copy

    def sent_z(n):
        return remote(terms_z.at[n], z1.at[n], n, at(y, line(n)[1], x))

    def sent_yx(n, s):
        y_of, x_of = turned(n)
        return remote(terms.at[n, pl.ds(2 * s, 2)], r1.at[n, pl.ds(2 * s, 2)], 7 + n * 4 + s, at(y_of, z, x_of))

    started = []

    def landed(copies):
        for copy in started:
            copy.wait_send()
        started.clear()
        for copy in copies:
            copy.wait_recv()
        started.extend(copies)

    def added(own_part, slots):
        acc = own_part
        for k in range(7):
            acc = acc + slots[k]
        return acc

    def step(s, carry):
        def of_z(n, carry):
            gather_z(n)
            sent_z(n).start()
            return carry

        def of_yx(n, carry):
            gather_yx(n, s)
            sent_yx(n, s).start()
            return carry

        lax.fori_loop(jnp.where(s == 0, 0, jnp.minimum(2 * s + 1, 7)), jnp.minimum(2 * s + 3, 7), of_z, 0)
        lax.fori_loop(0, 7, of_yx, 0)
        return carry

    lax.fori_loop(0, 4, step, 0)
    gather_z(7)

    def of_own(s, carry):
        gather_yx(7, s)
        return carry

    lax.fori_loop(0, 4, of_own, 0)
    landed([sent_z(n) for n in range(7)])
    total_z[...] = added(terms_z[7], z1)
    copies_z = []
    for n in range(7):
        y_of, x_of = turned(n)
        copies_z.append(start(total_z.at[y_of * 2 + x_of], z2.at[n], 35 + n, at(y_of, z, x_of)))
    landed([sent_yx(n, s) for s in range(4) for n in range(7)])
    total[...] = added(terms[7], r1)
    copies = []
    for n in range(7):
        other = line(n)[1]
        copies.append(start(total.at[other], r2.at[n], 42 + n, at(y, other, x)))
    landed(copies_z)
    acc_z = added(total_z[y * 2 + x], z2)
    landed(copies)
    acc = jnp.concatenate([acc_z, added(total[z], r2)], axis=0)
    mine = jnp.concatenate([acc[:, g * 32:g * 32 + 32].T for g in range(4)], axis=1)
    sketch[...] = mine
    whole[line_place] = mine
    landed([start(whole.at[line_place], whole.at[line_place], 49 + k - 1, x_line(k)) for k in range(1, 8)])
    every = [split(jnp.concatenate([whole[half * 4 + c] for c in range(4)], axis=0)) for half in range(2)]
    high, low = (jnp.concatenate([pieces[i] for pieces in every], axis=1) for i in range(2))
    rows16 = pl.ds(pl.multiple_of((line_place % 2) * 16, 16), 16)
    left = [split(whole[half * 4 + line_place // 2, rows16, :]) for half in range(2)]
    left_high, left_low = (jnp.concatenate([pieces[i] for pieces in left], axis=1) for i in range(2))
    part = lax.dot_general(left_high, high, NT, preferred_element_type=F32)
    part = part + lax.dot_general(left_high, low, NT, preferred_element_type=F32)
    part = part + lax.dot_general(left_low, high, NT, preferred_element_type=F32)
    r3[y] = part
    landed([start(r3.at[y], r3.at[y], 56 + k - 1, at((y + k) % 4, z, x)) for k in (2, 1, 3)])
    acc = (r3[0] + r3[1]) + (r3[2] + r3[3])
    r4[z] = acc
    landed([start(r4.at[z], r4.at[z], 59 + k - 1, at(y, (z + k) % 8, x)) for k in (4, 3, 5, 2, 6, 1, 7)])
    acc = ((r4[0] + r4[1]) + (r4[2] + r4[3])) + ((r4[4] + r4[5]) + (r4[6] + r4[7]))
    blocks[line_place] = acc * F32(1 / 8192)
    landed([start(blocks.at[line_place], blocks.at[line_place], 66 + k - 1, x_line(k)) for k in range(1, 8)])
    gram[...] = blocks[...].reshape(128, 128)
    for copy in started:
        copy.wait_send()


def per_device(table, signs, samples):
    hbm = pl.BlockSpec(memory_space=pltpu.HBM)
    vmem = pl.BlockSpec(memory_space=pltpu.VMEM)
    return pl.pallas_call(
        kernel,
        out_shape=(jax.ShapeDtypeStruct((32, 128), F32), jax.ShapeDtypeStruct((128, 128), F32)),
        in_specs=[hbm] * 3,
        out_specs=(vmem, vmem),
        scratch_shapes=[
            pltpu.VMEM((32, 16384), F32),
            pltpu.VMEM((128, 128), jnp.int32),
            pltpu.VMEM((128, 128), F32),
            pltpu.VMEM((64, 128), jnp.int32),
            pltpu.VMEM((32, 16384), F32),
            pltpu.VMEM((8, 256, 256), BF16),
            pltpu.VMEM((8, 256, 256), BF16),
            pltpu.VMEM((16384, 128), F32),
            pltpu.VMEM((64, 128), jnp.int32),
            pltpu.SMEM((64, 128), jnp.int32),
            pltpu.VMEM((64, 128), F32),
            pltpu.VMEM((8, 8, FIRST, 128), F32),
            pltpu.VMEM((7, 8, FIRST, 128), F32),
            pltpu.VMEM((8, FIRST, 128), F32),
            pltpu.VMEM((7, FIRST, 128), F32),
            pltpu.VMEM((8, 8, 32 - FIRST, 128), F32),
            pltpu.VMEM((7, 8, 32 - FIRST, 128), F32),
            pltpu.VMEM((8, 32 - FIRST, 128), F32),
            pltpu.VMEM((7, 32 - FIRST, 128), F32),
            pltpu.VMEM((8, 32, 128), F32),
            pltpu.VMEM((4, 16, 128), F32),
            pltpu.VMEM((8, 16, 128), F32),
            pltpu.VMEM((8, 16, 128), F32),
            pltpu.SemaphoreType.DMA((7,)),
            pltpu.SemaphoreType.DMA((73,)),
            pltpu.SemaphoreType.DMA((73,)),
        ],
        compiler_params=pltpu.CompilerParams(collective_id=0, has_side_effects=True, vmem_limit_bytes=40 * 2**20),
    )(*(pltpu.with_memory_space_constraint(a, pltpu.HBM) for a in (table, signs.reshape(128, 128), samples.reshape(64, 128))))


def solution(mesh):
    return jax.shard_map(
        per_device,
        mesh=mesh,
        in_specs=(P("col", "row"), P("row"), P()),
        out_specs=(P("col", "row"), P()),
        check_vma=False,
    )
```

```python
import jax
import jax.numpy as jnp
from jax import lax
from jax.experimental import pallas as pl
from jax.experimental.pallas import tpu as pltpu
from jax.sharding import PartitionSpec as P

F32 = jnp.float32
BF16 = jnp.bfloat16
MESH = pl.DeviceIdType.MESH
NT = (((1,), (1,)), ((), ()))
FIRST = 8


def butterflies(parts):
    parts = list(parts)
    step = 1
    while step < len(parts):
        for i in range(len(parts)):
            if not i & step:
                a, b = parts[i], parts[i | step]
                parts[i], parts[i | step] = a + b, a - b
        step *= 2
    return parts


def parity(v):
    for shift in (4, 2, 1):
        v = v ^ (v >> shift)
    return v & 1


def split(p):
    a = p.astype(BF16)
    return a, (p - a.astype(F32)).astype(BF16)


def kernel(
    table_hbm, signs_hbm, samples_hbm, sketch, gram,
    table, signs, flips, samples, xs, hi, lo, rows_of, index_v, index_s, sign_of, terms_z, z1, total_z, z2, terms, r1, total, r2,
    whole, r3, r4, blocks,
    load, send, recv,
):
    row = lax.axis_index("row")
    col = lax.axis_index("col")
    y, z, x = row // 16, (row // 2) % 8, row % 2
    line_place = x * 4 + col

    def at(y, z, x):
        return {"row": y * 16 + z * 2 + x}

    def x_line(k):
        other = (line_place + k) % 8
        return {"row": y * 16 + z * 2 + other // 4, "col": other % 4}

    partners = [(2, 1), (1, 1), (3, 1), (2, 0), (0, 1), (1, 0), (3, 0)]
    copies_in = [
        pltpu.make_async_copy(signs_hbm, signs, load.at[0]),
        pltpu.make_async_copy(table_hbm.at[pl.ds(0, 8)], table.at[pl.ds(0, 8)], load.at[1]),
        pltpu.make_async_copy(table_hbm.at[pl.ds(8, 8)], table.at[pl.ds(8, 8)], load.at[2]),
        pltpu.make_async_copy(samples_hbm, samples, load.at[3]),
        pltpu.make_async_copy(table_hbm.at[pl.ds(16, 8)], table.at[pl.ds(16, 8)], load.at[4]),
        pltpu.make_async_copy(table_hbm.at[pl.ds(24, 8)], table.at[pl.ds(24, 8)], load.at[5]),
    ]
    for copy in copies_in:
        copy.start()
    barrier = pltpu.get_barrier_semaphore()
    met = [at(y, (z + k) % 8, x) for k in (4, 3, 5, 2, 6, 1, 7)]
    met += [at((y + dy) % 4, z, (x + dx) % 2) for dy, dx in partners]
    met += [{"row": y * 16 + z * 2 + (x + dx) % 2, "col": (col + dc) % 4} for dx in range(2) for dc in range(1, 4)]
    for device in met:
        pl.semaphore_signal(barrier, inc=1, device_id=device, device_id_type=MESH)

    i = lax.broadcasted_iota(jnp.int32, (256, 256), 0)
    j = lax.broadcasted_iota(jnp.int32, (256, 256), 1)
    walsh = ((1 - 2 * parity(i & j)).astype(F32) * F32(1 / 1024)).astype(BF16)
    copies_in[0].wait()
    flips[...] = signs[...].astype(F32)
    for h in range(2):
        rows = slice(16 * h, 16 * h + 16)
        copies_in[1 + 3 * h].wait()
        copies_in[2 + 3 * h].wait()
        for t in range(2):
            for w in range(8):
                parts = []
                for u in range(8):
                    c = u * 16 + w * 2 + t
                    parts.append(table[rows, c * 128:(c + 1) * 128] * flips[c:c + 1, :])
                for u, p in enumerate(butterflies(parts)):
                    c = u * 16 + w * 2 + t
                    xs[rows, c * 128:(c + 1) * 128] = p
            for u in range(8):
                cs = [u * 16 + w * 2 + t for w in range(8)]
                parts = [xs[rows, c * 128:(c + 1) * 128] for c in cs]
                for w, p in enumerate(butterflies(parts)):
                    a, b = split(p)
                    put = slice(u * 32 + 16 * h, u * 32 + 16 * h + 16)
                    hi[w, put, t * 128:(t + 1) * 128] = a
                    lo[w, put, t * 128:(t + 1) * 128] = b
        if h == 0:
            copies_in[3].wait()
            local = samples[...] & 16383
            group = lax.broadcasted_iota(jnp.int32, (64, 128), 1) >> 5
            turn = (group - (local >> 11)) & 3
            index_v[...] = turn * 4096 + (local >> 13) * 2048 + (local & 2047)
            index_copy = pltpu.make_async_copy(index_v, index_s, load.at[6])
            index_copy.start()
            sign_of[...] = (1 - 2 * parity((samples[...] >> 14) & row)).astype(F32)
    for w in range(8):
        done = lax.dot_general(walsh, hi[w], NT, preferred_element_type=F32)
        done = done + lax.dot_general(walsh, lo[w], NT, preferred_element_type=F32)
        for half in range(2):
            tile = done[:, half * 128:half * 128 + 128]
            for k in range(4):
                put = k * 4096 + half * 2048 + w * 256
                rows_of[put:put + 256, :] = pltpu.roll(tile, 32 * k, 1) if k else tile
    index_copy.wait()
    pl.semaphore_wait(barrier, len(met))

    lane1 = lax.broadcasted_iota(jnp.int32, (1, 128), 1)
    below1 = [lane1 < 32, lane1 < 64, lane1 < 96]
    spread = (
        (lax.broadcasted_iota(jnp.int32, (128, 128), 0) >> 5) == (lax.broadcasted_iota(jnp.int32, (128, 128), 1) >> 5)
    ).astype(BF16)

    def gather(into, places, first, count, rs):
        padded = -(-count // 8) * 8
        mask = (lax.broadcasted_iota(jnp.int32, (padded, 128), 1) & 31) == (
            lax.broadcasted_iota(jnp.int32, (padded, 128), 0) + first
        )
        picked = [jnp.where(mask, sign_of[pl.ds(r, 1), :], F32(0)) for r in rs]
        factor = jnp.dot(jnp.concatenate(picked, axis=0).astype(BF16), spread, preferred_element_type=F32)
        for place, r in zip(places, rs):
            for p in range(count):
                v = [rows_of[pl.ds(index_s[r, g * 32 + first + p], 1), :] for g in range(4)]
                four = jnp.where(below1[0], v[0], jnp.where(below1[1], v[1], jnp.where(below1[2], v[2], v[3])))
                into[place + (pl.ds(p, 1), slice(None))] = four
        for i, place in enumerate(places):
            into[place] = into[place] * factor[i * padded:i * padded + count]

    def gather_z(n):
        _, other = line(n)

        def four(q, carry):
            gather(terms_z, [(n, q * 4 + e) for e in range(4)], 0, FIRST, [(2 * q + e // 2) * 16 + other * 2 + e % 2 for e in range(4)])
            return carry

        lax.fori_loop(0, 2, four, 0)

    def gather_yx(n, s):
        y_of, x_of = turned(n)
        gather(terms, [(n, 2 * s + j) for j in range(2)], FIRST, 32 - FIRST, [y_of * 16 + (2 * s + j) * 2 + x_of for j in range(2)])

    def line(n):
        k = jnp.where(n == 7, 0, (n + 4) % 8 + n // 4)
        return k, (z + k) % 8

    def turned(n):
        return (y + (7 - n) // 2) % 4, (x + (7 - n) % 2) % 2

    def remote(src, dst, place, device):
        return pltpu.make_async_remote_copy(
            src_ref=src, dst_ref=dst, send_sem=send.at[place], recv_sem=recv.at[place], device_id=device, device_id_type=MESH
        )

    def start(src, dst, place, device):
        copy = remote(src, dst, place, device)
        copy.start()
        return copy

    def sent_z(n):
        return remote(terms_z.at[n], z1.at[n], n, at(y, line(n)[1], x))

    def sent_yx(n, s):
        y_of, x_of = turned(n)
        return remote(terms.at[n, pl.ds(2 * s, 2)], r1.at[n, pl.ds(2 * s, 2)], 7 + n * 4 + s, at(y_of, z, x_of))

    started = []

    def landed(copies):
        for copy in started:
            copy.wait_send()
        started.clear()
        for copy in copies:
            copy.wait_recv()
        started.extend(copies)

    def added(own_part, slots):
        acc = own_part
        for k in range(7):
            acc = acc + slots[k]
        return acc

    def step(s, carry):
        def of_z(n, carry):
            gather_z(n)
            sent_z(n).start()
            return carry

        def of_yx(n, carry):
            gather_yx(n, s)
            sent_yx(n, s).start()
            return carry

        lax.fori_loop(jnp.where(s == 0, 0, jnp.minimum(2 * s + 1, 7)), jnp.minimum(2 * s + 3, 7), of_z, 0)
        lax.fori_loop(0, 7, of_yx, 0)
        return carry

    lax.fori_loop(0, 4, step, 0)
    gather_z(7)

    def of_own(s, carry):
        gather_yx(7, s)
        return carry

    lax.fori_loop(0, 4, of_own, 0)
    landed([sent_z(n) for n in range(7)])
    total_z[...] = added(terms_z[7], z1)
    copies_z = []
    for n in range(7):
        y_of, x_of = turned(n)
        copies_z.append(start(total_z.at[y_of * 2 + x_of], z2.at[n], 35 + n, at(y_of, z, x_of)))
    landed([sent_yx(n, s) for s in range(4) for n in range(7)])
    total[...] = added(terms[7], r1)
    copies = []
    for n in range(7):
        other = line(n)[1]
        copies.append(start(total.at[other], r2.at[n], 42 + n, at(y, other, x)))
    landed(copies_z)
    acc_z = added(total_z[y * 2 + x], z2)
    landed(copies)
    acc = jnp.concatenate([acc_z, added(total[z], r2)], axis=0)
    mine = jnp.concatenate([acc[:, g * 32:g * 32 + 32].T for g in range(4)], axis=1)
    sketch[...] = mine
    whole[line_place] = mine
    landed([start(whole.at[line_place], whole.at[line_place], 49 + k - 1, x_line(k)) for k in range(1, 8)])
    every = [split(jnp.concatenate([whole[half * 4 + c] for c in range(4)], axis=0)) for half in range(2)]
    high, low = (jnp.concatenate([pieces[i] for pieces in every], axis=1) for i in range(2))
    rows16 = pl.ds(pl.multiple_of((line_place % 2) * 16, 16), 16)
    left = [split(whole[half * 4 + line_place // 2, rows16, :]) for half in range(2)]
    left_high, left_low = (jnp.concatenate([pieces[i] for pieces in left], axis=1) for i in range(2))
    part = lax.dot_general(left_high, high, NT, preferred_element_type=F32)
    part = part + lax.dot_general(left_high, low, NT, preferred_element_type=F32)
    part = part + lax.dot_general(left_low, high, NT, preferred_element_type=F32)
    r3[y] = part
    landed([start(r3.at[y], r3.at[y], 56 + k - 1, at((y + k) % 4, z, x)) for k in (2, 1, 3)])
    acc = (r3[0] + r3[1]) + (r3[2] + r3[3])
    r4[z] = acc
    landed([start(r4.at[z], r4.at[z], 59 + k - 1, at(y, (z + k) % 8, x)) for k in (4, 3, 5, 2, 6, 1, 7)])
    acc = ((r4[0] + r4[1]) + (r4[2] + r4[3])) + ((r4[4] + r4[5]) + (r4[6] + r4[7]))
    blocks[line_place] = acc * F32(1 / 8192)
    landed([start(blocks.at[line_place], blocks.at[line_place], 66 + k - 1, x_line(k)) for k in range(1, 8)])
    gram[...] = blocks[...].reshape(128, 128)
    for copy in started:
        copy.wait_send()


def copy_kernel(a_in, b_in, a_out, b_out, sem):
    copies = [pltpu.make_async_copy(a_in, a_out, sem.at[0]), pltpu.make_async_copy(b_in, b_out, sem.at[1])]
    for copy in copies:
        copy.start()
    for copy in copies:
        copy.wait()


def per_device(table, signs, samples):
    hbm = pl.BlockSpec(memory_space=pltpu.HBM)
    vmem = pl.BlockSpec(memory_space=pltpu.VMEM)
    results = pl.pallas_call(
        kernel,
        out_shape=(pltpu.VMEM((32, 128), F32), pltpu.VMEM((128, 128), F32)),
        in_specs=[hbm] * 3,
        out_specs=(vmem, vmem),
        scratch_shapes=[
            pltpu.VMEM((32, 16384), F32),
            pltpu.VMEM((128, 128), jnp.int32),
            pltpu.VMEM((128, 128), F32),
            pltpu.VMEM((64, 128), jnp.int32),
            pltpu.VMEM((32, 16384), F32),
            pltpu.VMEM((8, 256, 256), BF16),
            pltpu.VMEM((8, 256, 256), BF16),
            pltpu.VMEM((16384, 128), F32),
            pltpu.VMEM((64, 128), jnp.int32),
            pltpu.SMEM((64, 128), jnp.int32),
            pltpu.VMEM((64, 128), F32),
            pltpu.VMEM((8, 8, FIRST, 128), F32),
            pltpu.VMEM((7, 8, FIRST, 128), F32),
            pltpu.VMEM((8, FIRST, 128), F32),
            pltpu.VMEM((7, FIRST, 128), F32),
            pltpu.VMEM((8, 8, 32 - FIRST, 128), F32),
            pltpu.VMEM((7, 8, 32 - FIRST, 128), F32),
            pltpu.VMEM((8, 32 - FIRST, 128), F32),
            pltpu.VMEM((7, 32 - FIRST, 128), F32),
            pltpu.VMEM((8, 32, 128), F32),
            pltpu.VMEM((4, 16, 128), F32),
            pltpu.VMEM((8, 16, 128), F32),
            pltpu.VMEM((8, 16, 128), F32),
            pltpu.SemaphoreType.DMA((7,)),
            pltpu.SemaphoreType.DMA((73,)),
            pltpu.SemaphoreType.DMA((73,)),
        ],
        compiler_params=pltpu.CompilerParams(collective_id=0, has_side_effects=True, vmem_limit_bytes=40 * 2**20),
    )(*(pltpu.with_memory_space_constraint(a, pltpu.HBM) for a in (table, signs.reshape(128, 128), samples.reshape(64, 128))))
    held = pl.BlockSpec(memory_space=pltpu.VMEM)
    return pl.pallas_call(
        copy_kernel,
        out_shape=(jax.ShapeDtypeStruct((32, 128), F32), jax.ShapeDtypeStruct((128, 128), F32)),
        in_specs=[held] * 2,
        out_specs=(hbm, hbm),
        scratch_shapes=[pltpu.SemaphoreType.DMA((2,))],
        compiler_params=pltpu.CompilerParams(vmem_limit_bytes=16 * 2**20),
    )(*results)


def solution(mesh):
    return jax.shard_map(
        per_device,
        mesh=mesh,
        in_specs=(P("col", "row"), P("row"), P()),
        out_specs=(P("col", "row"), P()),
        check_vma=False,
    )
```

```python
import jax
import jax.numpy as jnp
from jax import lax
from jax.experimental import pallas as pl
from jax.experimental.pallas import tpu as pltpu
from jax.sharding import PartitionSpec as P

F32 = jnp.float32
BF16 = jnp.bfloat16
MESH = pl.DeviceIdType.MESH
NT = (((1,), (1,)), ((), ()))
FIRST = 8


def butterflies(parts):
    parts = list(parts)
    step = 1
    while step < len(parts):
        for i in range(len(parts)):
            if not i & step:
                a, b = parts[i], parts[i | step]
                parts[i], parts[i | step] = a + b, a - b
        step *= 2
    return parts


def parity(v):
    for shift in (4, 2, 1):
        v = v ^ (v >> shift)
    return v & 1


def split(p):
    a = p.astype(BF16)
    return a, (p - a.astype(F32)).astype(BF16)


def kernel(
    table_hbm, signs_hbm, samples_hbm, sketch, gram,
    table, signs, flips, samples, xs, hi, lo, rows_of, index_v, index_s, sign_of, terms_z, z1, total_z, z2, terms, r1, total, r2,
    whole, r3, r4, blocks,
    load, send, recv,
):
    row = lax.axis_index("row")
    col = lax.axis_index("col")
    y, z, x = row // 16, (row // 2) % 8, row % 2
    line_place = x * 4 + col

    def at(y, z, x):
        return {"row": y * 16 + z * 2 + x}

    def x_line(k):
        other = (line_place + k) % 8
        return {"row": y * 16 + z * 2 + other // 4, "col": other % 4}

    partners = [(2, 1), (1, 1), (3, 1), (2, 0), (0, 1), (1, 0), (3, 0)]
    copies_in = [
        pltpu.make_async_copy(signs_hbm, signs, load.at[0]),
        pltpu.make_async_copy(table_hbm.at[pl.ds(0, 8)], table.at[pl.ds(0, 8)], load.at[1]),
        pltpu.make_async_copy(table_hbm.at[pl.ds(8, 8)], table.at[pl.ds(8, 8)], load.at[2]),
        pltpu.make_async_copy(samples_hbm, samples, load.at[3]),
        pltpu.make_async_copy(table_hbm.at[pl.ds(16, 8)], table.at[pl.ds(16, 8)], load.at[4]),
        pltpu.make_async_copy(table_hbm.at[pl.ds(24, 8)], table.at[pl.ds(24, 8)], load.at[5]),
    ]
    for copy in copies_in:
        copy.start()
    barrier = pltpu.get_barrier_semaphore()
    met = [at(y, (z + k) % 8, x) for k in (4, 3, 5, 2, 6, 1, 7)]
    met += [at((y + dy) % 4, z, (x + dx) % 2) for dy, dx in partners]
    met += [{"row": y * 16 + z * 2 + (x + dx) % 2, "col": (col + dc) % 4} for dx in range(2) for dc in range(1, 4)]
    for device in met:
        pl.semaphore_signal(barrier, inc=1, device_id=device, device_id_type=MESH)

    i = lax.broadcasted_iota(jnp.int32, (256, 256), 0)
    j = lax.broadcasted_iota(jnp.int32, (256, 256), 1)
    walsh = ((1 - 2 * parity(i & j)).astype(F32) * F32(1 / 1024)).astype(BF16)
    copies_in[0].wait()
    flips[...] = signs[...].astype(F32)
    for h in range(2):
        rows = slice(16 * h, 16 * h + 16)
        copies_in[1 + 3 * h].wait()
        copies_in[2 + 3 * h].wait()
        for t in range(2):
            for w in range(8):
                parts = []
                for u in range(8):
                    c = u * 16 + w * 2 + t
                    parts.append(table[rows, c * 128:(c + 1) * 128] * flips[c:c + 1, :])
                for u, p in enumerate(butterflies(parts)):
                    c = u * 16 + w * 2 + t
                    xs[rows, c * 128:(c + 1) * 128] = p
            for u in range(8):
                cs = [u * 16 + w * 2 + t for w in range(8)]
                parts = [xs[rows, c * 128:(c + 1) * 128] for c in cs]
                for w, p in enumerate(butterflies(parts)):
                    a, b = split(p)
                    put = slice(u * 32 + 16 * h, u * 32 + 16 * h + 16)
                    hi[w, put, t * 128:(t + 1) * 128] = a
                    lo[w, put, t * 128:(t + 1) * 128] = b
        if h == 0:
            copies_in[3].wait()
            local = samples[...] & 16383
            group = lax.broadcasted_iota(jnp.int32, (64, 128), 1) >> 5
            turn = (group - (local >> 11)) & 3
            index_v[...] = turn * 4096 + (local >> 13) * 2048 + (local & 2047)
            index_copy = pltpu.make_async_copy(index_v, index_s, load.at[6])
            index_copy.start()
            sign_of[...] = (1 - 2 * parity((samples[...] >> 14) & row)).astype(F32)
    for w in range(8):
        done = lax.dot_general(walsh, hi[w], NT, preferred_element_type=F32)
        done = done + lax.dot_general(walsh, lo[w], NT, preferred_element_type=F32)
        for half in range(2):
            tile = done[:, half * 128:half * 128 + 128]
            for k in range(4):
                put = k * 4096 + half * 2048 + w * 256
                rows_of[put:put + 256, :] = pltpu.roll(tile, 32 * k, 1) if k else tile
    index_copy.wait()
    pl.semaphore_wait(barrier, len(met))

    lane1 = lax.broadcasted_iota(jnp.int32, (1, 128), 1)
    below1 = [lane1 < 32, lane1 < 64, lane1 < 96]
    spread = (
        (lax.broadcasted_iota(jnp.int32, (128, 128), 0) >> 5) == (lax.broadcasted_iota(jnp.int32, (128, 128), 1) >> 5)
    ).astype(BF16)

    def gather(into, places, first, count, rs):
        padded = -(-count // 8) * 8
        mask = (lax.broadcasted_iota(jnp.int32, (padded, 128), 1) & 31) == (
            lax.broadcasted_iota(jnp.int32, (padded, 128), 0) + first
        )
        picked = [jnp.where(mask, sign_of[pl.ds(r, 1), :], F32(0)) for r in rs]
        factor = jnp.dot(jnp.concatenate(picked, axis=0).astype(BF16), spread, preferred_element_type=F32)
        for place, r in zip(places, rs):
            for p in range(count):
                v = [rows_of[pl.ds(index_s[r, g * 32 + first + p], 1), :] for g in range(4)]
                four = jnp.where(below1[0], v[0], jnp.where(below1[1], v[1], jnp.where(below1[2], v[2], v[3])))
                into[place + (pl.ds(p, 1), slice(None))] = four
        for i, place in enumerate(places):
            into[place] = into[place] * factor[i * padded:i * padded + count]

    def gather_z(n):
        _, other = line(n)

        def four(q, carry):
            gather(terms_z, [(n, q * 4 + e) for e in range(4)], 0, FIRST, [(2 * q + e // 2) * 16 + other * 2 + e % 2 for e in range(4)])
            return carry

        lax.fori_loop(0, 2, four, 0)

    def gather_yx(n, s):
        y_of, x_of = turned(n)
        gather(terms, [(n, 2 * s + j) for j in range(2)], FIRST, 32 - FIRST, [y_of * 16 + (2 * s + j) * 2 + x_of for j in range(2)])

    def line(n):
        k = jnp.where(n == 7, 0, (n + 4) % 8 + n // 4)
        return k, (z + k) % 8

    def turned(n):
        return (y + (7 - n) // 2) % 4, (x + (7 - n) % 2) % 2

    def remote(src, dst, place, device):
        return pltpu.make_async_remote_copy(
            src_ref=src, dst_ref=dst, send_sem=send.at[place], recv_sem=recv.at[place], device_id=device, device_id_type=MESH
        )

    def start(src, dst, place, device):
        copy = remote(src, dst, place, device)
        copy.start()
        return copy

    def sent_z(n):
        return remote(terms_z.at[n], z1.at[n], n, at(y, line(n)[1], x))

    def sent_yx(n, s):
        y_of, x_of = turned(n)
        return remote(terms.at[n, pl.ds(2 * s, 2)], r1.at[n, pl.ds(2 * s, 2)], 7 + n * 4 + s, at(y_of, z, x_of))

    started = []

    def landed(copies):
        for copy in started:
            copy.wait_send()
        started.clear()
        for copy in copies:
            copy.wait_recv()
        started.extend(copies)

    def added(own_part, slots):
        acc = own_part
        for k in range(7):
            acc = acc + slots[k]
        return acc

    def step(s, carry):
        def of_z(n, carry):
            gather_z(n)
            sent_z(n).start()
            return carry

        def of_yx(n, carry):
            gather_yx(n, s)
            sent_yx(n, s).start()
            return carry

        lax.fori_loop(jnp.where(s == 0, 0, jnp.minimum(2 * s + 1, 7)), jnp.minimum(2 * s + 3, 7), of_z, 0)
        lax.fori_loop(0, 7, of_yx, 0)
        return carry

    lax.fori_loop(0, 4, step, 0)
    gather_z(7)

    def of_own(s, carry):
        gather_yx(7, s)
        return carry

    lax.fori_loop(0, 4, of_own, 0)
    landed([sent_z(n) for n in range(7)])
    total_z[...] = added(terms_z[7], z1)
    copies_z = []
    for n in range(7):
        y_of, x_of = turned(n)
        copies_z.append(start(total_z.at[y_of * 2 + x_of], z2.at[n], 35 + n, at(y_of, z, x_of)))
    landed([sent_yx(n, s) for s in range(4) for n in range(7)])
    total[...] = added(terms[7], r1)
    copies = []
    for n in range(7):
        other = line(n)[1]
        copies.append(start(total.at[other], r2.at[n], 42 + n, at(y, other, x)))
    landed(copies_z)
    acc_z = added(total_z[y * 2 + x], z2)
    landed(copies)
    acc = jnp.concatenate([acc_z, added(total[z], r2)], axis=0)
    mine = jnp.concatenate([acc[:, g * 32:g * 32 + 32].T for g in range(4)], axis=1)
    sketch[...] = mine
    whole[col] = mine
    landed([start(whole.at[col], whole.at[col], 49 + k - 1, {"col": (col + k) % 4}) for k in range(1, 4)])
    high, low = split(whole[0:4].reshape(128, 128))
    left_high, left_low = split(mine)
    part = lax.dot_general(left_high, high, NT, preferred_element_type=F32)
    part = part + lax.dot_general(left_high, low, NT, preferred_element_type=F32)
    part = part + lax.dot_general(left_low, high, NT, preferred_element_type=F32)
    r3[y] = part
    landed([start(r3.at[y], r3.at[y], 56 + k - 1, at((y + k) % 4, z, x)) for k in (2, 1, 3)])
    acc = (r3[0] + r3[1]) + (r3[2] + r3[3])
    r4[z] = acc
    landed([start(r4.at[z], r4.at[z], 59 + k - 1, at(y, (z + k) % 8, x)) for k in (4, 3, 5, 2, 6, 1, 7)])
    acc = ((r4[0] + r4[1]) + (r4[2] + r4[3])) + ((r4[4] + r4[5]) + (r4[6] + r4[7]))
    blocks[line_place] = acc * F32(1 / 8192)
    landed([start(blocks.at[line_place], blocks.at[line_place], 66 + k - 1, x_line(k)) for k in range(1, 8)])
    gram[...] = (blocks[0:4] + blocks[4:8]).reshape(128, 128)
    for copy in started:
        copy.wait_send()


def copy_kernel(a_in, b_in, a_out, b_out, sem):
    copies = [pltpu.make_async_copy(a_in, a_out, sem.at[0]), pltpu.make_async_copy(b_in, b_out, sem.at[1])]
    for copy in copies:
        copy.start()
    for copy in copies:
        copy.wait()


def per_device(table, signs, samples):
    hbm = pl.BlockSpec(memory_space=pltpu.HBM)
    vmem = pl.BlockSpec(memory_space=pltpu.VMEM)
    results = pl.pallas_call(
        kernel,
        out_shape=(pltpu.VMEM((32, 128), F32), pltpu.VMEM((128, 128), F32)),
        in_specs=[hbm] * 3,
        out_specs=(vmem, vmem),
        scratch_shapes=[
            pltpu.VMEM((32, 16384), F32),
            pltpu.VMEM((128, 128), jnp.int32),
            pltpu.VMEM((128, 128), F32),
            pltpu.VMEM((64, 128), jnp.int32),
            pltpu.VMEM((32, 16384), F32),
            pltpu.VMEM((8, 256, 256), BF16),
            pltpu.VMEM((8, 256, 256), BF16),
            pltpu.VMEM((16384, 128), F32),
            pltpu.VMEM((64, 128), jnp.int32),
            pltpu.SMEM((64, 128), jnp.int32),
            pltpu.VMEM((64, 128), F32),
            pltpu.VMEM((8, 8, FIRST, 128), F32),
            pltpu.VMEM((7, 8, FIRST, 128), F32),
            pltpu.VMEM((8, FIRST, 128), F32),
            pltpu.VMEM((7, FIRST, 128), F32),
            pltpu.VMEM((8, 8, 32 - FIRST, 128), F32),
            pltpu.VMEM((7, 8, 32 - FIRST, 128), F32),
            pltpu.VMEM((8, 32 - FIRST, 128), F32),
            pltpu.VMEM((7, 32 - FIRST, 128), F32),
            pltpu.VMEM((8, 32, 128), F32),
            pltpu.VMEM((4, 32, 128), F32),
            pltpu.VMEM((8, 32, 128), F32),
            pltpu.VMEM((8, 32, 128), F32),
            pltpu.SemaphoreType.DMA((7,)),
            pltpu.SemaphoreType.DMA((73,)),
            pltpu.SemaphoreType.DMA((73,)),
        ],
        compiler_params=pltpu.CompilerParams(collective_id=0, has_side_effects=True, vmem_limit_bytes=40 * 2**20),
    )(*(pltpu.with_memory_space_constraint(a, pltpu.HBM) for a in (table, signs.reshape(128, 128), samples.reshape(64, 128))))
    held = pl.BlockSpec(memory_space=pltpu.VMEM)
    return pl.pallas_call(
        copy_kernel,
        out_shape=(jax.ShapeDtypeStruct((32, 128), F32), jax.ShapeDtypeStruct((128, 128), F32)),
        in_specs=[held] * 2,
        out_specs=(hbm, hbm),
        scratch_shapes=[pltpu.SemaphoreType.DMA((2,))],
        compiler_params=pltpu.CompilerParams(vmem_limit_bytes=16 * 2**20),
    )(*results)


def solution(mesh):
    return jax.shard_map(
        per_device,
        mesh=mesh,
        in_specs=(P("col", "row"), P("row"), P()),
        out_specs=(P("col", "row"), P()),
        check_vma=False,
    )
```

```python
import jax
import jax.numpy as jnp
from jax import lax
from jax.experimental import pallas as pl
from jax.experimental.pallas import tpu as pltpu
from jax.sharding import PartitionSpec as P

F32 = jnp.float32
BF16 = jnp.bfloat16
MESH = pl.DeviceIdType.MESH
NT = (((1,), (1,)), ((), ()))
FIRST = 8


def butterflies(parts):
    parts = list(parts)
    step = 1
    while step < len(parts):
        for i in range(len(parts)):
            if not i & step:
                a, b = parts[i], parts[i | step]
                parts[i], parts[i | step] = a + b, a - b
        step *= 2
    return parts


def parity(v):
    for shift in (4, 2, 1):
        v = v ^ (v >> shift)
    return v & 1


def split(p):
    a = p.astype(BF16)
    return a, (p - a.astype(F32)).astype(BF16)


def kernel(
    table_hbm, signs_hbm, samples_hbm, sketch, gram,
    table, signs, flips, samples, xs, hi, lo, rows_of, index_v, index_s, sign_of, terms_z, z1, total_z, z2, terms, r1, total, r2,
    whole, r3, r4, blocks,
    load, send, recv,
):
    row = lax.axis_index("row")
    col = lax.axis_index("col")
    y, z, x = row // 16, (row // 2) % 8, row % 2
    line_place = x * 4 + col

    def at(y, z, x):
        return {"row": y * 16 + z * 2 + x}

    def x_line(k):
        other = (line_place + k) % 8
        return {"row": y * 16 + z * 2 + other // 4, "col": other % 4}

    partners = [(2, 1), (1, 1), (3, 1), (2, 0), (0, 1), (1, 0), (3, 0)]
    copies_in = [
        pltpu.make_async_copy(signs_hbm, signs, load.at[0]),
        pltpu.make_async_copy(table_hbm.at[pl.ds(0, 8)], table.at[pl.ds(0, 8)], load.at[1]),
        pltpu.make_async_copy(table_hbm.at[pl.ds(8, 8)], table.at[pl.ds(8, 8)], load.at[2]),
        pltpu.make_async_copy(samples_hbm, samples, load.at[3]),
        pltpu.make_async_copy(table_hbm.at[pl.ds(16, 8)], table.at[pl.ds(16, 8)], load.at[4]),
        pltpu.make_async_copy(table_hbm.at[pl.ds(24, 8)], table.at[pl.ds(24, 8)], load.at[5]),
    ]
    for copy in copies_in:
        copy.start()
    barrier = pltpu.get_barrier_semaphore()
    met = [at(y, (z + k) % 8, x) for k in (4, 3, 5, 2, 6, 1, 7)]
    met += [at((y + dy) % 4, z, (x + dx) % 2) for dy, dx in partners]
    met += [{"row": y * 16 + z * 2 + (x + dx) % 2, "col": (col + dc) % 4} for dx in range(2) for dc in range(1, 4)]
    for device in met:
        pl.semaphore_signal(barrier, inc=1, device_id=device, device_id_type=MESH)

    i = lax.broadcasted_iota(jnp.int32, (256, 256), 0)
    j = lax.broadcasted_iota(jnp.int32, (256, 256), 1)
    walsh = ((1 - 2 * parity(i & j)).astype(F32) * F32(1 / 1024)).astype(BF16)
    copies_in[0].wait()
    flips[...] = signs[...].astype(F32)
    for h in range(2):
        rows = slice(16 * h, 16 * h + 16)
        copies_in[1 + 3 * h].wait()
        copies_in[2 + 3 * h].wait()
        for t in range(2):
            for w in range(8):
                parts = []
                for u in range(8):
                    c = u * 16 + w * 2 + t
                    parts.append(table[rows, c * 128:(c + 1) * 128] * flips[c:c + 1, :])
                for u, p in enumerate(butterflies(parts)):
                    c = u * 16 + w * 2 + t
                    xs[rows, c * 128:(c + 1) * 128] = p
            for u in range(8):
                cs = [u * 16 + w * 2 + t for w in range(8)]
                parts = [xs[rows, c * 128:(c + 1) * 128] for c in cs]
                for w, p in enumerate(butterflies(parts)):
                    a, b = split(p)
                    put = slice(u * 32 + 16 * h, u * 32 + 16 * h + 16)
                    hi[w, put, t * 128:(t + 1) * 128] = a
                    lo[w, put, t * 128:(t + 1) * 128] = b
        if h == 0:
            copies_in[3].wait()
            local = samples[...] & 16383
            group = lax.broadcasted_iota(jnp.int32, (64, 128), 1) >> 5
            turn = (group - (local >> 11)) & 3
            index_v[...] = turn * 4096 + (local >> 13) * 2048 + (local & 2047)
            index_copy = pltpu.make_async_copy(index_v, index_s, load.at[6])
            index_copy.start()
            sign_of[...] = (1 - 2 * parity((samples[...] >> 14) & row)).astype(F32)
    for w in range(8):
        done = lax.dot_general(walsh, hi[w], NT, preferred_element_type=F32)
        done = done + lax.dot_general(walsh, lo[w], NT, preferred_element_type=F32)
        for half in range(2):
            tile = done[:, half * 128:half * 128 + 128]
            for k in range(4):
                put = k * 4096 + half * 2048 + w * 256
                rows_of[put:put + 256, :] = pltpu.roll(tile, 32 * k, 1) if k else tile
    index_copy.wait()
    pl.semaphore_wait(barrier, len(met))

    lane1 = lax.broadcasted_iota(jnp.int32, (1, 128), 1)
    below1 = [lane1 < 32, lane1 < 64, lane1 < 96]
    spread = (
        (lax.broadcasted_iota(jnp.int32, (128, 128), 0) >> 5) == (lax.broadcasted_iota(jnp.int32, (128, 128), 1) >> 5)
    ).astype(BF16)

    def gather(into, places, first, count, rs):
        padded = -(-count // 8) * 8
        mask = (lax.broadcasted_iota(jnp.int32, (padded, 128), 1) & 31) == (
            lax.broadcasted_iota(jnp.int32, (padded, 128), 0) + first
        )
        picked = [jnp.where(mask, sign_of[pl.ds(r, 1), :], F32(0)) for r in rs]
        factor = jnp.dot(jnp.concatenate(picked, axis=0).astype(BF16), spread, preferred_element_type=F32)
        for place, r in zip(places, rs):
            for p in range(count):
                v = [rows_of[pl.ds(index_s[r, g * 32 + first + p], 1), :] for g in range(4)]
                four = jnp.where(below1[0], v[0], jnp.where(below1[1], v[1], jnp.where(below1[2], v[2], v[3])))
                into[place + (pl.ds(p, 1), slice(None))] = four
        for i, place in enumerate(places):
            into[place] = into[place] * factor[i * padded:i * padded + count]

    def gather_z(n):
        _, other = line(n)

        def four(q, carry):
            gather(terms_z, [(n, q * 4 + e) for e in range(4)], 0, FIRST, [(2 * q + e // 2) * 16 + other * 2 + e % 2 for e in range(4)])
            return carry

        lax.fori_loop(0, 2, four, 0)

    def gather_yx(n, s):
        y_of, x_of = turned(n)
        gather(terms, [(n, 2 * s + j) for j in range(2)], FIRST, 32 - FIRST, [y_of * 16 + (2 * s + j) * 2 + x_of for j in range(2)])

    def line(n):
        k = jnp.where(n == 7, 0, (n + 4) % 8 + n // 4)
        return k, (z + k) % 8

    def turned(n):
        return (y + (7 - n) // 2) % 4, (x + (7 - n) % 2) % 2

    def remote(src, dst, place, device):
        return pltpu.make_async_remote_copy(
            src_ref=src, dst_ref=dst, send_sem=send.at[place], recv_sem=recv.at[place], device_id=device, device_id_type=MESH
        )

    def start(src, dst, place, device):
        copy = remote(src, dst, place, device)
        copy.start()
        return copy

    def sent_z(n):
        return remote(terms_z.at[n], z1.at[n], n, at(y, line(n)[1], x))

    def sent_yx(n, s):
        y_of, x_of = turned(n)
        return remote(terms.at[n, pl.ds(2 * s, 2)], r1.at[n, pl.ds(2 * s, 2)], 7 + n * 4 + s, at(y_of, z, x_of))

    started = []

    def landed(copies):
        for copy in started:
            copy.wait_send()
        started.clear()
        for copy in copies:
            copy.wait_recv()
        started.extend(copies)

    def added(own_part, slots):
        acc = own_part
        for k in range(7):
            acc = acc + slots[k]
        return acc

    def step(s, carry):
        def of_z(n, carry):
            gather_z(n)
            sent_z(n).start()
            return carry

        def of_yx(n, carry):
            gather_yx(n, s)
            sent_yx(n, s).start()
            return carry

        lax.fori_loop(jnp.where(s == 0, 0, jnp.minimum(2 * s + 1, 7)), jnp.minimum(2 * s + 3, 7), of_z, 0)
        lax.fori_loop(0, 7, of_yx, 0)
        return carry

    lax.fori_loop(0, 4, step, 0)
    gather_z(7)

    def of_own(s, carry):
        gather_yx(7, s)
        return carry

    lax.fori_loop(0, 4, of_own, 0)
    landed([sent_z(n) for n in range(7)])
    total_z[...] = added(terms_z[7], z1)
    copies_z = []
    for n in range(7):
        y_of, x_of = turned(n)
        copies_z.append(start(total_z.at[y_of * 2 + x_of], z2.at[n], 35 + n, at(y_of, z, x_of)))
    landed([sent_yx(n, s) for s in range(4) for n in range(7)])
    total[...] = added(terms[7], r1)
    copies = []
    for n in range(7):
        other = line(n)[1]
        copies.append(start(total.at[other], r2.at[n], 42 + n, at(y, other, x)))
    landed(copies_z)
    acc_z = added(total_z[y * 2 + x], z2)
    landed(copies)
    acc = jnp.concatenate([acc_z, added(total[z], r2)], axis=0)
    mine = jnp.concatenate([acc[:, g * 32:g * 32 + 32].T for g in range(4)], axis=1)
    sketch[...] = mine
    whole[col] = mine
    landed([start(whole.at[col], whole.at[col], 49 + k - 1, {"col": (col + k) % 4}) for k in range(1, 4)])
    high, low = split(whole[0:4].reshape(128, 128))
    left_high, left_low = split(mine)
    part = lax.dot_general(left_high, high, NT, preferred_element_type=F32)
    part = part + lax.dot_general(left_high, low, NT, preferred_element_type=F32)
    part = part + lax.dot_general(left_low, high, NT, preferred_element_type=F32)
    place = y * 2 + x
    r3[place] = part
    landed([start(r3.at[place], r3.at[place], 52 + n, (lambda o: at(o[0], z, o[1]))(turned(n))) for n in range(7)])
    acc = ((r3[0] + r3[1]) + (r3[2] + r3[3])) + ((r3[4] + r3[5]) + (r3[6] + r3[7]))
    r4[z] = acc
    landed([start(r4.at[z], r4.at[z], 59 + k - 1, at(y, (z + k) % 8, x)) for k in (4, 3, 5, 2, 6, 1, 7)])
    acc = ((r4[0] + r4[1]) + (r4[2] + r4[3])) + ((r4[4] + r4[5]) + (r4[6] + r4[7]))
    blocks[col] = acc * F32(1 / 8192)
    landed([start(blocks.at[col], blocks.at[col], 66 + k - 1, {"col": (col + k) % 4}) for k in range(1, 4)])
    gram[...] = blocks[0:4].reshape(128, 128)
    for copy in started:
        copy.wait_send()


def copy_kernel(a_in, b_in, a_out, b_out, sem):
    copies = [pltpu.make_async_copy(a_in, a_out, sem.at[0]), pltpu.make_async_copy(b_in, b_out, sem.at[1])]
    for copy in copies:
        copy.start()
    for copy in copies:
        copy.wait()


def per_device(table, signs, samples):
    hbm = pl.BlockSpec(memory_space=pltpu.HBM)
    vmem = pl.BlockSpec(memory_space=pltpu.VMEM)
    results = pl.pallas_call(
        kernel,
        out_shape=(pltpu.VMEM((32, 128), F32), pltpu.VMEM((128, 128), F32)),
        in_specs=[hbm] * 3,
        out_specs=(vmem, vmem),
        scratch_shapes=[
            pltpu.VMEM((32, 16384), F32),
            pltpu.VMEM((128, 128), jnp.int32),
            pltpu.VMEM((128, 128), F32),
            pltpu.VMEM((64, 128), jnp.int32),
            pltpu.VMEM((32, 16384), F32),
            pltpu.VMEM((8, 256, 256), BF16),
            pltpu.VMEM((8, 256, 256), BF16),
            pltpu.VMEM((16384, 128), F32),
            pltpu.VMEM((64, 128), jnp.int32),
            pltpu.SMEM((64, 128), jnp.int32),
            pltpu.VMEM((64, 128), F32),
            pltpu.VMEM((8, 8, FIRST, 128), F32),
            pltpu.VMEM((7, 8, FIRST, 128), F32),
            pltpu.VMEM((8, FIRST, 128), F32),
            pltpu.VMEM((7, FIRST, 128), F32),
            pltpu.VMEM((8, 8, 32 - FIRST, 128), F32),
            pltpu.VMEM((7, 8, 32 - FIRST, 128), F32),
            pltpu.VMEM((8, 32 - FIRST, 128), F32),
            pltpu.VMEM((7, 32 - FIRST, 128), F32),
            pltpu.VMEM((8, 32, 128), F32),
            pltpu.VMEM((8, 32, 128), F32),
            pltpu.VMEM((8, 32, 128), F32),
            pltpu.VMEM((8, 32, 128), F32),
            pltpu.SemaphoreType.DMA((7,)),
            pltpu.SemaphoreType.DMA((73,)),
            pltpu.SemaphoreType.DMA((73,)),
        ],
        compiler_params=pltpu.CompilerParams(collective_id=0, has_side_effects=True, vmem_limit_bytes=40 * 2**20),
    )(*(pltpu.with_memory_space_constraint(a, pltpu.HBM) for a in (table, signs.reshape(128, 128), samples.reshape(64, 128))))
    held = pl.BlockSpec(memory_space=pltpu.VMEM)
    return pl.pallas_call(
        copy_kernel,
        out_shape=(jax.ShapeDtypeStruct((32, 128), F32), jax.ShapeDtypeStruct((128, 128), F32)),
        in_specs=[held] * 2,
        out_specs=(hbm, hbm),
        scratch_shapes=[pltpu.SemaphoreType.DMA((2,))],
        compiler_params=pltpu.CompilerParams(vmem_limit_bytes=16 * 2**20),
    )(*results)


def solution(mesh):
    return jax.shard_map(
        per_device,
        mesh=mesh,
        in_specs=(P("col", "row"), P("row"), P()),
        out_specs=(P("col", "row"), P()),
        check_vma=False,
    )
```

```python
import jax
import jax.numpy as jnp
from jax import lax
from jax.experimental import pallas as pl
from jax.experimental.pallas import tpu as pltpu
from jax.sharding import PartitionSpec as P

F32 = jnp.float32
BF16 = jnp.bfloat16
MESH = pl.DeviceIdType.MESH
NT = (((1,), (1,)), ((), ()))
FIRST = 8


def butterflies(parts):
    parts = list(parts)
    step = 1
    while step < len(parts):
        for i in range(len(parts)):
            if not i & step:
                a, b = parts[i], parts[i | step]
                parts[i], parts[i | step] = a + b, a - b
        step *= 2
    return parts


def parity(v):
    for shift in (4, 2, 1):
        v = v ^ (v >> shift)
    return v & 1


def split(p):
    a = p.astype(BF16)
    return a, (p - a.astype(F32)).astype(BF16)


def kernel(
    table_hbm, signs_hbm, samples_hbm, sketch, gram,
    table, signs, flips, samples, xs, hi, lo, rows_of, index_v, index_s, sign_of, terms_z, z1, total_z, z2, terms, r1, total, r2,
    whole, r3, r4, blocks,
    load, send, recv,
):
    row = lax.axis_index("row")
    col = lax.axis_index("col")
    y, z, x = row // 16, (row // 2) % 8, row % 2
    line_place = x * 4 + col

    def at(y, z, x):
        return {"row": y * 16 + z * 2 + x}

    def x_line(k):
        other = (line_place + k) % 8
        return {"row": y * 16 + z * 2 + other // 4, "col": other % 4}

    partners = [(2, 1), (1, 1), (3, 1), (2, 0), (0, 1), (1, 0), (3, 0)]
    copies_in = [
        pltpu.make_async_copy(signs_hbm, signs, load.at[0]),
        pltpu.make_async_copy(table_hbm.at[pl.ds(0, 8)], table.at[pl.ds(0, 8)], load.at[1]),
        pltpu.make_async_copy(table_hbm.at[pl.ds(8, 8)], table.at[pl.ds(8, 8)], load.at[2]),
        pltpu.make_async_copy(samples_hbm, samples, load.at[3]),
        pltpu.make_async_copy(table_hbm.at[pl.ds(16, 8)], table.at[pl.ds(16, 8)], load.at[4]),
        pltpu.make_async_copy(table_hbm.at[pl.ds(24, 8)], table.at[pl.ds(24, 8)], load.at[5]),
    ]
    for copy in copies_in:
        copy.start()
    barrier = pltpu.get_barrier_semaphore()
    met = [at(y, (z + k) % 8, x) for k in (4, 3, 5, 2, 6, 1, 7)]
    met += [at((y + dy) % 4, z, (x + dx) % 2) for dy, dx in partners]
    met += [{"row": y * 16 + z * 2 + (x + dx) % 2, "col": (col + dc) % 4} for dx in range(2) for dc in range(1, 4)]
    for device in met:
        pl.semaphore_signal(barrier, inc=1, device_id=device, device_id_type=MESH)

    i = lax.broadcasted_iota(jnp.int32, (256, 256), 0)
    j = lax.broadcasted_iota(jnp.int32, (256, 256), 1)
    walsh = ((1 - 2 * parity(i & j)).astype(F32) * F32(1 / 1024)).astype(BF16)
    copies_in[0].wait()
    flips[...] = signs[...].astype(F32)
    for h in range(2):
        rows = slice(16 * h, 16 * h + 16)
        copies_in[1 + 3 * h].wait()
        copies_in[2 + 3 * h].wait()
        for t in range(2):
            for u in range(8):
                parts = []
                for w in range(8):
                    c = u * 16 + w * 2 + t
                    parts.append(table[rows, c * 128:(c + 1) * 128] * flips[c:c + 1, :])
                for w, p in enumerate(butterflies(parts)):
                    c = u * 16 + w * 2 + t
                    xs[rows, c * 128:(c + 1) * 128] = p
        if h == 0:
            copies_in[3].wait()
            local = samples[...] & 16383
            group = lax.broadcasted_iota(jnp.int32, (64, 128), 1) >> 5
            turn = (group - (local >> 11)) & 3
            index_v[...] = turn * 4096 + (local >> 13) * 2048 + (local & 2047)
            index_copy = pltpu.make_async_copy(index_v, index_s, load.at[6])
            index_copy.start()
            sign_of[...] = (1 - 2 * parity((samples[...] >> 14) & row)).astype(F32)
    def split_part(w):
        for h in range(2):
            rows = slice(16 * h, 16 * h + 16)
            for t in range(2):
                cs = [u * 16 + w * 2 + t for u in range(8)]
                for u, p in enumerate(butterflies([xs[rows, c * 128:(c + 1) * 128] for c in cs])):
                    a, b = split(p)
                    put = slice(u * 32 + 16 * h, u * 32 + 16 * h + 16)
                    hi[w, put, t * 128:(t + 1) * 128] = a
                    lo[w, put, t * 128:(t + 1) * 128] = b

    split_part(0)
    for w in range(8):
        if w < 7:
            split_part(w + 1)
        done = lax.dot_general(walsh, hi[w], NT, preferred_element_type=F32)
        done = done + lax.dot_general(walsh, lo[w], NT, preferred_element_type=F32)
        for half in range(2):
            tile = done[:, half * 128:half * 128 + 128]
            for k in range(4):
                put = k * 4096 + half * 2048 + w * 256
                rows_of[put:put + 256, :] = pltpu.roll(tile, 32 * k, 1) if k else tile
    index_copy.wait()
    pl.semaphore_wait(barrier, len(met))

    lane1 = lax.broadcasted_iota(jnp.int32, (1, 128), 1)
    below1 = [lane1 < 32, lane1 < 64, lane1 < 96]
    spread = (
        (lax.broadcasted_iota(jnp.int32, (128, 128), 0) >> 5) == (lax.broadcasted_iota(jnp.int32, (128, 128), 1) >> 5)
    ).astype(BF16)

    def gather(into, places, first, count, rs):
        padded = -(-count // 8) * 8
        mask = (lax.broadcasted_iota(jnp.int32, (padded, 128), 1) & 31) == (
            lax.broadcasted_iota(jnp.int32, (padded, 128), 0) + first
        )
        picked = [jnp.where(mask, sign_of[pl.ds(r, 1), :], F32(0)) for r in rs]
        factor = jnp.dot(jnp.concatenate(picked, axis=0).astype(BF16), spread, preferred_element_type=F32)
        for place, r in zip(places, rs):
            for p in range(count):
                v = [rows_of[pl.ds(index_s[r, g * 32 + first + p], 1), :] for g in range(4)]
                four = jnp.where(below1[0], v[0], jnp.where(below1[1], v[1], jnp.where(below1[2], v[2], v[3])))
                into[place + (pl.ds(p, 1), slice(None))] = four
        for i, place in enumerate(places):
            into[place] = into[place] * factor[i * padded:i * padded + count]

    def gather_z(n):
        _, other = line(n)

        def four(q, carry):
            gather(terms_z, [(n, q * 4 + e) for e in range(4)], 0, FIRST, [(2 * q + e // 2) * 16 + other * 2 + e % 2 for e in range(4)])
            return carry

        lax.fori_loop(0, 2, four, 0)

    def gather_yx(n, s):
        y_of, x_of = turned(n)
        gather(terms, [(n, 2 * s + j) for j in range(2)], FIRST, 32 - FIRST, [y_of * 16 + (2 * s + j) * 2 + x_of for j in range(2)])

    def line(n):
        k = jnp.where(n == 7, 0, (n + 4) % 8 + n // 4)
        return k, (z + k) % 8

    def turned(n):
        return (y + (7 - n) // 2) % 4, (x + (7 - n) % 2) % 2

    def remote(src, dst, place, device):
        return pltpu.make_async_remote_copy(
            src_ref=src, dst_ref=dst, send_sem=send.at[place], recv_sem=recv.at[place], device_id=device, device_id_type=MESH
        )

    def start(src, dst, place, device):
        copy = remote(src, dst, place, device)
        copy.start()
        return copy

    def sent_z(n):
        return remote(terms_z.at[n], z1.at[n], n, at(y, line(n)[1], x))

    def sent_yx(n, s):
        y_of, x_of = turned(n)
        return remote(terms.at[n, pl.ds(2 * s, 2)], r1.at[n, pl.ds(2 * s, 2)], 7 + n * 4 + s, at(y_of, z, x_of))

    started = []

    def landed(copies):
        for copy in started:
            copy.wait_send()
        started.clear()
        for copy in copies:
            copy.wait_recv()
        started.extend(copies)

    def added(own_part, slots):
        acc = own_part
        for k in range(7):
            acc = acc + slots[k]
        return acc

    def step(s, carry):
        def of_z(n, carry):
            gather_z(n)
            sent_z(n).start()
            return carry

        def of_yx(n, carry):
            gather_yx(n, s)
            sent_yx(n, s).start()
            return carry

        lax.fori_loop(jnp.where(s == 0, 0, jnp.minimum(2 * s + 1, 7)), jnp.minimum(2 * s + 3, 7), of_z, 0)
        lax.fori_loop(0, 7, of_yx, 0)
        return carry

    lax.fori_loop(0, 4, step, 0)
    gather_z(7)

    def of_own(s, carry):
        gather_yx(7, s)
        return carry

    lax.fori_loop(0, 4, of_own, 0)
    landed([sent_z(n) for n in range(7)])
    total_z[...] = added(terms_z[7], z1)
    copies_z = []
    for n in range(7):
        y_of, x_of = turned(n)
        copies_z.append(start(total_z.at[y_of * 2 + x_of], z2.at[n], 35 + n, at(y_of, z, x_of)))
    landed([sent_yx(n, s) for s in range(4) for n in range(7)])
    total[...] = added(terms[7], r1)
    copies = []
    for n in range(7):
        other = line(n)[1]
        copies.append(start(total.at[other], r2.at[n], 42 + n, at(y, other, x)))
    landed(copies_z)
    acc_z = added(total_z[y * 2 + x], z2)
    landed(copies)
    acc = jnp.concatenate([acc_z, added(total[z], r2)], axis=0)
    mine = jnp.concatenate([acc[:, g * 32:g * 32 + 32].T for g in range(4)], axis=1)
    sketch[...] = mine
    whole[col] = mine
    landed([start(whole.at[col], whole.at[col], 49 + k - 1, {"col": (col + k) % 4}) for k in range(1, 4)])
    high, low = split(whole[0:4].reshape(128, 128))
    left_high, left_low = split(mine)
    part = lax.dot_general(left_high, high, NT, preferred_element_type=F32)
    part = part + lax.dot_general(left_high, low, NT, preferred_element_type=F32)
    part = part + lax.dot_general(left_low, high, NT, preferred_element_type=F32)
    r3[y] = part
    landed([start(r3.at[y], r3.at[y], 56 + k - 1, at((y + k) % 4, z, x)) for k in (2, 1, 3)])
    acc = (r3[0] + r3[1]) + (r3[2] + r3[3])
    r4[z] = acc
    landed([start(r4.at[z], r4.at[z], 59 + k - 1, at(y, (z + k) % 8, x)) for k in (4, 3, 5, 2, 6, 1, 7)])
    acc = ((r4[0] + r4[1]) + (r4[2] + r4[3])) + ((r4[4] + r4[5]) + (r4[6] + r4[7]))
    blocks[line_place] = acc * F32(1 / 8192)
    landed([start(blocks.at[line_place], blocks.at[line_place], 66 + k - 1, x_line(k)) for k in range(1, 8)])
    gram[...] = (blocks[0:4] + blocks[4:8]).reshape(128, 128)
    for copy in started:
        copy.wait_send()


def copy_kernel(a_in, b_in, a_out, b_out, sem):
    copies = [pltpu.make_async_copy(a_in, a_out, sem.at[0]), pltpu.make_async_copy(b_in, b_out, sem.at[1])]
    for copy in copies:
        copy.start()
    for copy in copies:
        copy.wait()


def per_device(table, signs, samples):
    hbm = pl.BlockSpec(memory_space=pltpu.HBM)
    vmem = pl.BlockSpec(memory_space=pltpu.VMEM)
    results = pl.pallas_call(
        kernel,
        out_shape=(pltpu.VMEM((32, 128), F32), pltpu.VMEM((128, 128), F32)),
        in_specs=[hbm] * 3,
        out_specs=(vmem, vmem),
        scratch_shapes=[
            pltpu.VMEM((32, 16384), F32),
            pltpu.VMEM((128, 128), jnp.int32),
            pltpu.VMEM((128, 128), F32),
            pltpu.VMEM((64, 128), jnp.int32),
            pltpu.VMEM((32, 16384), F32),
            pltpu.VMEM((8, 256, 256), BF16),
            pltpu.VMEM((8, 256, 256), BF16),
            pltpu.VMEM((16384, 128), F32),
            pltpu.VMEM((64, 128), jnp.int32),
            pltpu.SMEM((64, 128), jnp.int32),
            pltpu.VMEM((64, 128), F32),
            pltpu.VMEM((8, 8, FIRST, 128), F32),
            pltpu.VMEM((7, 8, FIRST, 128), F32),
            pltpu.VMEM((8, FIRST, 128), F32),
            pltpu.VMEM((7, FIRST, 128), F32),
            pltpu.VMEM((8, 8, 32 - FIRST, 128), F32),
            pltpu.VMEM((7, 8, 32 - FIRST, 128), F32),
            pltpu.VMEM((8, 32 - FIRST, 128), F32),
            pltpu.VMEM((7, 32 - FIRST, 128), F32),
            pltpu.VMEM((8, 32, 128), F32),
            pltpu.VMEM((4, 32, 128), F32),
            pltpu.VMEM((8, 32, 128), F32),
            pltpu.VMEM((8, 32, 128), F32),
            pltpu.SemaphoreType.DMA((7,)),
            pltpu.SemaphoreType.DMA((73,)),
            pltpu.SemaphoreType.DMA((73,)),
        ],
        compiler_params=pltpu.CompilerParams(collective_id=0, has_side_effects=True, vmem_limit_bytes=40 * 2**20),
    )(*(pltpu.with_memory_space_constraint(a, pltpu.HBM) for a in (table, signs.reshape(128, 128), samples.reshape(64, 128))))
    held = pl.BlockSpec(memory_space=pltpu.VMEM)
    return pl.pallas_call(
        copy_kernel,
        out_shape=(jax.ShapeDtypeStruct((32, 128), F32), jax.ShapeDtypeStruct((128, 128), F32)),
        in_specs=[held] * 2,
        out_specs=(hbm, hbm),
        scratch_shapes=[pltpu.SemaphoreType.DMA((2,))],
        compiler_params=pltpu.CompilerParams(vmem_limit_bytes=16 * 2**20),
    )(*results)


def solution(mesh):
    return jax.shard_map(
        per_device,
        mesh=mesh,
        in_specs=(P("col", "row"), P("row"), P()),
        out_specs=(P("col", "row"), P()),
        check_vma=False,
    )
```
